32 devices in a mesh: dp: 8 (over y, x, core), expert: 4 (over z).
Axes of the slice: x: 2, y: 2, z: 4, core: 2. Of those that a mesh axis runs over, the one named last changes fastest.
Arguments:
- tokens: bfloat16 [512, 2048], P(('dp', 'expert')), may hold values from -6 to 6
- out_grad: bfloat16 [512, 2048], P(('dp', 'expert')), may hold values from -6 to 6
- gate_weights: bfloat16 [512, 2], P(('dp', 'expert')), may hold values from 0.049804688 to 1
- expert_ids: int32 [512, 2], P(('dp', 'expert')), may hold values from 0 to 3, all different within a row; in each aligned block of 16 rows (0 to 15, 16 to 31, ...) at most 10 rows name the same one
- swapped: int32 [4], replicated, may hold values from 0 to 1, as said below
- up_weight: bfloat16 [4, 2048, 384], P('expert'), may hold values from -0.125 to 0.125
- down_weight: bfloat16 [4, 384, 2048], P('expert'), may hold values from -0.3125 to 0.3125
Outputs:
- layer_out: bfloat16 [512, 2048], P(('dp', 'expert'))
- token_grad: bfloat16 [512, 2048], P(('dp', 'expert'))
- up_grad: float32 [4, 2048, 384], P('expert', 'dp')
- down_grad: float32 [4, 384, 2048], P('expert', 'dp')
The draws below stay inside these ranges and needn't reach their ends.
Inputs may be any that keep to these rules, and one draw needn't show every extreme that they name: swapped[s] equals swapped[(s + 2) mod 4]; swapped[0] is 1. `expert_ids`: A token's 2 experts differ; at most 10 of the tokens of one device name one expert, and that many in some device.
All inputs are finite; a program needn't handle non-finite values.
Results may differ from the reference program's by a relative error of at most 0.023.
Values may be sent and summed in bfloat16 or wider, within the bound.
A program may use at most 64 MiB of HBM per device.

```python
import math
import jax
import jax.numpy as jnp
import numpy as np
from jax import lax

D = 2048
FW = 384
TOK_DEV = 16
EXPERTS = 4
TOP = 2
CAP = 10
TOKENS = 512
N_DP = 8
N_EXPERT = 4


def draw_swapped(key, part):
    half = EXPERTS // 2
    key_base = jax.random.fold_in(key, 11)
    base = jax.random.randint(key_base, (half,), 0, 2).astype(jnp.int32)
    first = jnp.arange(half, dtype=jnp.int32) == 0
    base = jnp.where(first, 1, base).astype(jnp.int32)
    return jnp.concatenate([base, base]).astype(jnp.int32)


def spiked(drawn, rng, source, target, blocks, factor):
    owner, partner = [(jnp.arange(drawn.shape[position]) // (drawn.shape[position] // blocks)).reshape([-1 if axis == position else 1 for axis in range(drawn.ndim)]) for position in (source, target)]
    chosen = jax.random.permutation(rng, blocks)[partner]
    strong = (owner == chosen) | (owner == (partner + blocks // 2) % blocks)
    return jnp.where(strong, factor * drawn, drawn)


def level_of(stream_key, dims, pieces, low, high):
    loudness = 1.0
    for axis_at, parts in pieces:
        steps = jax.random.uniform(jax.random.fold_in(jax.random.fold_in(stream_key, 6), axis_at), (parts,), jnp.float32, low / len(pieces), high / len(pieces))
        loudness = loudness * jnp.repeat(jnp.exp(steps), dims[axis_at] // parts).reshape((-1,) + (1,) * (len(dims) - 1 - axis_at))
    return loudness


def shared_out(stream_key, own, number, rows, count, top, limit, lean):
    sequence = jax.random.permutation(stream_key, count)
    packed, usual = portions_of(count, rows * top, limit, lean, True), portions_of(count, rows * top, limit, lean, False)
    places = jnp.arange(count)

    def named(lengths, offset_by):
        used = int((lengths > 0).sum())
        fixed = max(1, used // 4)
        shifted = fixed + (places - fixed + offset_by * (used - fixed)) % max(1, count - fixed)
        return jnp.zeros((count,), jnp.int32).at[sequence[jnp.where(places < fixed, places, shifted)]].set(jnp.asarray(lengths, jnp.int32))

    lengths = jnp.where(number % 4 == 0, named(packed, number // 4), named(usual, number - number // 4 - 1))
    mixed = jax.random.permutation(jax.random.fold_in(own, 3), count)
    giver, sink = mixed[0:count // 2 * 2:2], mixed[1:count // 2 * 2:2]
    slack = jnp.minimum(lengths[giver] - 1, limit - lengths[sink]) // 2
    slack = jnp.where((giver == sequence[0]) | (sink == sequence[0]) | (lengths[sink] == 0), 0, jnp.maximum(slack, 0))
    shifted = jax.random.randint(jax.random.fold_in(own, 4), (count // 2,), 0, 1 << 20) % (slack + 1)
    lengths = lengths.at[giver].add(-shifted).at[sink].add(shifted)
    labels = jnp.searchsorted(jnp.cumsum(lengths), jnp.arange(rows * top), side="right").astype(jnp.int32)
    grid = labels.reshape(top, rows).T
    grid = grid[jax.random.permutation(jax.random.fold_in(own, 1), rows)]
    offset_by = jax.random.randint(jax.random.fold_in(own, 2), (rows, 1), 0, top)
    return jnp.take_along_axis(grid, (jnp.arange(top)[None, :] + offset_by) % top, axis=1)


def portions_of(number_of, total, limit, lean, full):
    loads = [(1 << 20) // math.isqrt(standing ** lean) + 1 for standing in range(1, number_of + 1)]
    largest = limit if full else min(limit, max(-(-total // number_of), total * loads[0] // sum(loads)))
    least = 1 if total - largest >= number_of - 1 else 0
    counts, surplus = [largest] + [least] * (number_of - 1), total - largest - least * (number_of - 1)
    while surplus > 0:
        free = [i for i in range(1, number_of) if counts[i] < largest] or [i for i in range(1, number_of) if counts[i] < limit]
        mass, left = sum([loads[i] for i in free]), surplus
        for i in free:
            more = min(limit - counts[i], max(1, left * loads[i] // mass), surplus)
            counts[i] = counts[i] + more
            surplus = surplus - more
    return np.array(counts)


def normal_values(rng, dims, scale, limit, shards=(), kind=jnp.bfloat16):
    result = jax.random.normal(rng, dims, jnp.float32) * scale
    if len(shards) > 0:
        result = level_of(rng, dims, shards, -0.22, 0.18) * result
    return jnp.clip(result, min=-limit, max=limit).astype(kind)


def noise_with(rng, shape, scale, most, shards, heavy, kind=jnp.bfloat16):
    drawn = scale * jax.random.normal(rng, shape, jnp.float32)
    if shards:
        drawn = drawn * level_of(rng, shape, shards, -0.22, 0.18)
    return jnp.clip(spiked(drawn, jax.random.fold_in(rng, 3), *heavy), -most, most).astype(kind)


def setup_inputs(seed: int = 0) -> dict:
    key_list = jax.random.split(jax.random.key(seed), 8)
    tokens = noise_with(key_list[0], (TOKENS, D), 1.0, 6.0, ((0, 32),), (0, 1, 32, 2.75))
    out_grad = normal_values(key_list[1], (TOKENS, D), 1.0, 6.0, ((0, 32),))
    gate_weights = jnp.clip(jnp.exp(math.log(1.0) - 2.9996462 * jax.random.uniform(key_list[2], (TOKENS, TOP), jnp.float32) ** level_of(key_list[2], (TOKENS, TOP), ((0, 32),), -0.2, 0.2)), 0.049804688, 1.0).astype(jnp.bfloat16)
    expert_ids_keys = jax.random.split(jax.random.fold_in(key_list[3], 1), TOKENS // TOK_DEV)
    expert_ids_turns = jax.random.permutation(jax.random.fold_in(key_list[3], 3), TOKENS // TOK_DEV)
    expert_ids = jax.vmap(lambda own, number: shared_out(jax.random.fold_in(key_list[3], 2), own, number, TOK_DEV, EXPERTS, TOP, CAP, 1))(expert_ids_keys, expert_ids_turns).reshape((TOKENS, TOP))
    swapped = draw_swapped(jax.random.fold_in(key_list[7], 71), 0)
    up_weight = normal_values(key_list[5], (EXPERTS, D, FW), D ** -0.5, 0.125, ((0, 4),))
    down_weight = normal_values(key_list[6], (EXPERTS, FW, D), FW ** -0.5, 0.3125, ((0, 4),))
    return dict(tokens=tokens, out_grad=out_grad, gate_weights=gate_weights, expert_ids=expert_ids, swapped=swapped, up_weight=up_weight, down_weight=down_weight)


def positions(ids):
    flat = ids.reshape(-1)
    onehot = (flat[:, None] == jnp.arange(EXPERTS, dtype=jnp.int32)[None, :]).astype(jnp.int32)
    before = jnp.cumsum(onehot, axis=0) - onehot
    return jnp.sum(before * onehot, axis=1).reshape(ids.shape).astype(jnp.int32)


def reference(tokens, out_grad, gate_weights, expert_ids, swapped, up_weight, down_weight):
    rows = N_EXPERT * CAP
    high = lax.Precision.HIGHEST
    up_f = up_weight.astype(jnp.float32)
    down_f = down_weight.astype(jnp.float32)

    def group(carry, inputs):
        total_up, total_down = carry
        x, og, gates, ids = inputs
        pos = jax.vmap(positions)(ids)
        source = jnp.arange(N_EXPERT, dtype=jnp.int32)[:, None, None]
        row = (source * CAP + pos).astype(jnp.int32)
        x_rep = jnp.broadcast_to(x[:, :, None, :], (N_EXPERT, TOK_DEV, TOP, D)).astype(jnp.float32)
        og_rep = jnp.broadcast_to(og[:, :, None, :], (N_EXPERT, TOK_DEV, TOP, D)).astype(jnp.float32)
        x_buf = jnp.zeros((EXPERTS, rows, D), jnp.float32).at[ids, row].set(x_rep)
        og_buf = jnp.zeros((EXPERTS, rows, D), jnp.float32).at[ids, row].set(og_rep)
        g_buf = jnp.zeros((EXPERTS, rows), jnp.float32).at[ids, row].set(gates.astype(jnp.float32))
        h = jnp.einsum("erd,edf->erf", x_buf, up_f, precision=high)
        act = jax.nn.silu(h).astype(jnp.bfloat16).astype(jnp.float32)
        y = jnp.einsum("erf,efd->erd", act, down_f, precision=high).astype(jnp.bfloat16)
        dy = (g_buf[:, :, None] * og_buf).astype(jnp.bfloat16).astype(jnp.float32)
        dact = jnp.einsum("erd,efd->erf", dy, down_f, precision=high)
        sig = jax.nn.sigmoid(h)
        dh = (dact * sig * (1.0 + h * (1.0 - sig))).astype(jnp.bfloat16).astype(jnp.float32)
        dx = jnp.einsum("erf,edf->erd", dh, up_f, precision=high).astype(jnp.bfloat16)
        part_down = jnp.einsum("erf,erd->efd", act, dy, precision=high)
        part_up = jnp.einsum("erd,erf->edf", x_buf, dh, precision=high)
        part_down = lax.optimization_barrier(part_down.astype(jnp.bfloat16)).astype(jnp.float32)
        part_up = lax.optimization_barrier(part_up.astype(jnp.bfloat16)).astype(jnp.float32)
        y_pick = y[ids, row].astype(jnp.float32)
        out = jnp.sum(gates.astype(jnp.float32)[..., None] * y_pick, axis=2).astype(jnp.bfloat16)
        grad_tok = jnp.sum(dx[ids, row].astype(jnp.float32), axis=2).astype(jnp.bfloat16)
        return (total_up + part_up, total_down + part_down), (out, grad_tok)

    xs = (tokens.reshape(N_DP, N_EXPERT, TOK_DEV, D),
          out_grad.reshape(N_DP, N_EXPERT, TOK_DEV, D),
          gate_weights.reshape(N_DP, N_EXPERT, TOK_DEV, TOP),
          expert_ids.reshape(N_DP, N_EXPERT, TOK_DEV, TOP))
    init = (jnp.zeros((EXPERTS, D, FW), jnp.float32), jnp.zeros((EXPERTS, FW, D), jnp.float32))
    (total_up, total_down), (outs, grads) = lax.scan(group, init, xs)
    slots = jnp.arange(EXPERTS, dtype=jnp.int32)
    flags = swapped[slots]
    holder = jnp.where(flags == 1, (slots + EXPERTS // 2) % EXPERTS, slots).astype(jnp.int32)
    layer_out = outs.reshape(TOKENS, D)
    token_grad = grads.reshape(TOKENS, D)
    return layer_out, token_grad, total_up[holder], total_down[holder]
```

```python
import functools

import jax
import jax.numpy as jnp
from jax import lax
from jax.experimental import pallas as pl
from jax.experimental.pallas import tpu as pltpu
from jax.sharding import PartitionSpec as P

BF = jnp.bfloat16
F32 = jnp.float32


def by_collectives(tokens, out_grad, gate_weights, expert_ids, swapped, up_weight, down_weight):
    owners = lax.axis_size("expert")
    mine = lax.axis_index("expert")
    width = tokens.shape[1]
    lanes = jnp.arange(128, dtype=jnp.int32)
    hit = expert_ids[:, :, None] == lanes[None, None, :]
    gates = jnp.sum(jnp.where(hit, gate_weights.astype(F32)[:, :, None], 0.0), axis=1).astype(BF)
    packed = jnp.concatenate([tokens, out_grad, gates], axis=1)
    full = lax.all_gather(packed, "expert", axis=0, tiled=True)
    x, og, gates = full[:, :width], full[:, width : 2 * width], full[:, 2 * width :]
    gates = gates.astype(F32)
    flag = lax.dynamic_slice_in_dim(swapped, mine, 1, 0)[0] == 1
    held = jnp.where(flag, (mine + owners // 2) % owners, mine)

    def column(e):
        return jnp.sum(jnp.where(lanes[None, :] == e, gates, 0.0), axis=1, keepdims=True)

    gate = column(mine)
    up, down = up_weight[0], down_weight[0]
    dy = (gate * og.astype(F32)).astype(BF)
    hidden = jnp.dot(x, up, preferred_element_type=F32)
    d_active = lax.dot_general(dy, down, (((1,), (1,)), ((), ())), preferred_element_type=F32)
    sigma = jax.nn.sigmoid(hidden)
    active = jnp.where(gate > 0, hidden * sigma, 0.0).astype(BF)
    d_hidden = (d_active * sigma * (1.0 + hidden * (1.0 - sigma))).astype(BF)
    other = lax.ppermute(
        jnp.concatenate([active, d_hidden], axis=1),
        "expert",
        [(i, (i + owners // 2) % owners) for i in range(owners)],
    )
    y = jnp.dot(active, down, preferred_element_type=F32).astype(BF).astype(F32)
    dx = lax.dot_general(d_hidden, up, (((1,), (1,)), ((), ())), preferred_element_type=F32)
    back = jnp.concatenate([(gate * y).astype(BF), dx.astype(BF)], axis=1)
    back = lax.psum_scatter(back, "expert", scatter_dimension=0, tiled=True)
    fw = active.shape[1]
    act_h = jnp.where(flag, other[:, :fw], active)
    dh_h = jnp.where(flag, other[:, fw:], d_hidden)
    dy_h = (column(held) * og.astype(F32)).astype(BF)
    over = (((0,), (0,)), ((), ()))
    part_up = lax.dot_general(x, dh_h, over, preferred_element_type=F32).astype(BF)
    part_down = lax.dot_general(act_h, dy_h, over, preferred_element_type=F32).astype(BF)
    sum_up = lax.psum_scatter(part_up, "dp", scatter_dimension=0, tiled=True).astype(F32)
    sum_down = lax.psum_scatter(part_down, "dp", scatter_dimension=0, tiled=True).astype(F32)
    return back[:, :width], back[:, width:], sum_up[None], sum_down[None]


NT = (((1,), (1,)), ((), ()))
TN = (((0,), (0,)), ((), ()))


def dot(a, b, dims=(((1,), (0,)), ((), ()))):
    return lax.dot_general(a, b, dims, preferred_element_type=F32)


X_IN, OG_IN, X_OWN, OG_OWN, X_REST, OG_REST = 0, 3, 6, 7, 8, 9
SWAP_ACT, SWAP_DH, ACT_IN, ACT_TWIN, DH_IN, DH_TWIN, DOWN, Y, DX = 10, 11, 12, 15, 16, 19, 20, 21, 22
ARRIVALS = 23
(
    S_X,
    S_OG,
    S_X_OWN,
    S_OG_OWN,
    S_X_REST,
    S_OG_REST,
    S_SWAP_ACT,
    S_SWAP_DH,
    S_ACT,
    S_DH,
    S_DOWN,
    S_Y,
    S_DX,
) = range(13)
DEPARTURES = 13


def kernel(
    swapped_ref,
    tok_ref,
    og_ref,
    gate_ref,
    ids_ref,
    up_ref,
    down_ref,
    out_ref,
    tgrad_ref,
    ugrad_ref,
    dgrad_ref,
    xs,
    ogs,
    up_buf,
    down_buf,
    x_in,
    og_in,
    own_act,
    own_dh,
    other_act,
    other_dh,
    act_all,
    dh_all,
    y_out,
    y_in,
    dx_out,
    dx_in,
    down_out,
    down_in,
    load,
    left,
    came,
):
    owners, groups = 4, 8
    tok, width = tok_ref.shape
    fw = up_ref.shape[2]
    part, depth, half, eighth = width // groups, fw // groups, width // 2, width // 8
    count = owners * tok
    me = lax.axis_index("expert")
    group = lax.axis_index("dp")
    chip, core = group // 2, lax.rem(group, 2)
    middle = jnp.logical_or(me == 1, me == 2)
    twin = 2 * chip + 1 - core

    def peer(f):
        return 2 * lax.rem(chip + f % 4, 4) + lax.rem(core + f // 4, 2)

    def back(f):
        return f // 4 * 4 + (4 - f % 4) % 4

    def cols(p):
        return pl.ds(pl.multiple_of(p * part, 128), part)

    def z_peer(k):
        return lax.rem(me + k, owners)

    def send(src, dst, s, r, **where):
        return pltpu.make_async_remote_copy(
            src_ref=src,
            dst_ref=dst,
            send_sem=left.at[s],
            recv_sem=came.at[r],
            device_id=where,
            device_id_type=pl.DeviceIdType.MESH,
        )

    def arrived(dst, r):
        send(dst, dst, 0, r, dp=twin).wait_recv()

    def departed(src, s):
        send(src, src, s, 0, dp=twin).wait_send()

    barrier = pltpu.get_barrier_semaphore()
    for k in range(1, owners):
        pl.semaphore_signal(
            barrier, inc=1, device_id={"expert": z_peer(k)}, device_id_type=pl.DeviceIdType.MESH
        )
    for f in range(1, groups):
        pl.semaphore_signal(
            barrier, inc=1, device_id={"dp": peer(f)}, device_id_type=pl.DeviceIdType.MESH
        )
    loads = [
        pltpu.make_async_copy(tok_ref, xs.at[0, :, pl.ds(0, width)], load.at[0]),
        pltpu.make_async_copy(og_ref, ogs.at[0], load.at[1]),
        pltpu.make_async_copy(up_ref.at[0], up_buf, load.at[2]),
        pltpu.make_async_copy(down_ref.at[0], down_buf, load.at[3]),
    ]
    for copy in loads:
        copy.start()
    lines = lax.broadcasted_iota(jnp.int32, (128, tok), 0)
    dense = jnp.zeros((128, tok), F32)
    for k in range(ids_ref.shape[0]):
        hit = ids_ref[k : k + 1, :] == lines
        dense += jnp.where(hit, gate_ref[k : k + 1, :].astype(F32), 0.0)
    eye = (
        lax.broadcasted_iota(jnp.int32, (128, 128), 0)
        == lax.broadcasted_iota(jnp.int32, (128, 128), 1)
    ).astype(BF)
    own_gates = dot(dense.astype(BF), eye, TN)
    xs[0, :, width:] = own_gates.astype(BF)

    def column(v, e):
        lane = lax.broadcasted_iota(jnp.int32, v.shape, 1)
        return jnp.sum(jnp.where(lane == e, v, 0.0), axis=1, keepdims=True)

    def before(hits):
        rows = hits.shape[0]
        r = lax.broadcasted_iota(jnp.int32, (rows, rows), 0)
        c = lax.broadcasted_iota(jnp.int32, (rows, rows), 1)
        earlier = jnp.logical_and(c < r, c // tok == r // tok).astype(BF)
        return dot(earlier, hits.astype(BF))

    own_hits = (own_gates > 0).astype(F32)
    own_rank = before(own_hits)
    lane = lax.broadcasted_iota(jnp.int32, (tok, count), 1).astype(F32)
    main_pick = [jnp.zeros((tok, count), F32) for _ in range(2)]
    rest_pick = [jnp.zeros((tok, count), F32) for _ in range(8)]
    for j in range(owners):
        e = z_peer(j)
        hit, rank = column(own_hits, e), column(own_rank, e)
        low = jnp.where(rank < 8, hit, 0.0)
        high = hit - low
        for h in range(2):
            main_pick[h] += jnp.where(lane == tok * j + 8 * h + rank, low, 0.0)
        for q in range(8):
            rest_pick[q] += jnp.where(lane == tok * j + 2 * q + rank - 8, high, 0.0)
    main_pick = jnp.concatenate(main_pick, axis=0).astype(BF)
    rest_pick = jnp.concatenate(rest_pick, axis=0).astype(BF)
    c = lax.broadcasted_iota(jnp.int32, (count, count), 1)
    perm = (
        lax.broadcasted_iota(jnp.int32, (count, count), 0)
        == 16 * ((c >> 1) & 3) + 2 * (c >> 3) + (c & 1)
    ).astype(BF)

    def fold(y, dst):
        for k in range(owners):
            rows = y[8 * k : 8 * k + 8]
            dst[k, :, :half] = jnp.concatenate([rows[:, :half], rows[:, half:]], axis=0).astype(BF)
        rest = jnp.concatenate(
            [y[32:40, eighth * j : eighth * (j + 1)] for j in range(8)], axis=0
        ).astype(BF)
        dst[:, :, half:] = dot(perm, rest).astype(BF).reshape(owners, tok, eighth)

    def unfold(src, dst):
        main = dot(main_pick, src[:, :, :half].reshape(count, half))
        rest = dot(rest_pick, src[:, :, half:].reshape(count, eighth))
        for q in range(8):
            h, at = q // 4, q % 4 * eighth
            dst[:, q * eighth : (q + 1) * eighth] = (
                main[tok * h : tok * (h + 1), at : at + eighth] + rest[tok * q : tok * (q + 1)]
            ).astype(BF)

    flag = swapped_ref[me]
    loads[0].wait()
    loads[1].wait()
    pl.semaphore_wait(barrier, owners + groups - 2)

    hops = ((2, me < 2), (-2, me > 1), (1, me < 3), (-1, me > 0))

    def gather(buf, s, r):
        for d, there in hops:
            slot = -d % owners

            @pl.when(there)
            def _():
                send(
                    buf.at[0], buf.at[slot], s, r + slot - 1, expert=lax.rem(me + d + owners, owners)
                ).start()

    def pass_on(buf, s, r):
        arrived(buf.at[2], r + 1)
        slot = 1 + 2 * lax.rem(me, 2)

        @pl.when(middle)
        def _():
            pltpu.make_async_remote_copy(
                src_ref=buf.at[2],
                dst_ref=buf.at[slot],
                send_sem=left.at[s],
                recv_sem=came.at[r + slot - 1],
                device_id={"expert": lax.rem(3 * (me + 3), owners)},
                device_id_type=pl.DeviceIdType.MESH,
            ).start()

    def spread(buf, dst, at, s, r):
        for f in range(1, groups):
            p = peer(f)
            send(buf.at[at, :, cols(p)], dst.at[back(f), at], s, r, dp=p).start()
        dst[0, at] = buf[at, :, cols(group)]

    rest = pl.ds(1, owners - 1)

    def spread_rest(buf, dst, s, r):
        for f in range(1, groups):
            p = peer(f)
            send(buf.at[rest, :, cols(p)], dst.at[back(f), rest], s, r, dp=p).start()
        dst[0, 1:] = buf[1:, :, cols(group)]

    gather(xs, S_X, X_IN)
    gather(ogs, S_OG, OG_IN)
    spread(xs, x_in, 0, S_X_OWN, X_OWN)
    spread(ogs, og_in, 0, S_OG_OWN, OG_OWN)
    pass_on(xs, S_X, X_IN)
    arrived(xs.at[1], X_IN)
    arrived(xs.at[3], X_IN + 2)
    spread_rest(xs, x_in, S_X_REST, X_REST)
    pass_on(ogs, S_OG, OG_IN)

    gates = xs[:, :, width:].reshape(count, 128).astype(F32)
    gate = column(gates, me)
    hits = (gates > 0).astype(F32)
    hit, rank = column(hits, me), column(before(hits), me)
    block = (lax.broadcasted_iota(jnp.int32, (count, 1), 0) // tok).astype(F32)
    row = jnp.where(rank < 8, 8 * block + rank, 32 + 2 * block + rank - 8)
    lane = lax.broadcasted_iota(jnp.int32, (count, 48), 1).astype(F32)
    pack = jnp.where(lane == row, hit, 0.0).astype(BF)

    loads[2].wait()
    up = up_buf[...]
    hidden = dot(xs[:, :, :width].reshape(count, width), up)
    sigma = 1.0 / (1.0 + jnp.exp(-hidden))
    active = (gate * (hidden * sigma)).astype(BF)
    slope = sigma * (1.0 + hidden * (1.0 - sigma))
    own_act[...] = active
    partner = lax.rem(me + 2, owners)
    send(own_act, other_act, S_SWAP_ACT, SWAP_ACT, expert=partner).start()
    loads[3].wait()
    down = down_buf[...]
    fold(dot(dot(pack, active, TN).astype(BF), down), y_out)

    arrived(ogs.at[1], OG_IN)
    arrived(ogs.at[3], OG_IN + 2)
    spread_rest(ogs, og_in, S_OG_REST, OG_REST)
    dy = (gate * ogs[...].reshape(count, width).astype(F32)).astype(BF)
    d_hidden = (dot(dy, down, NT) * slope).astype(BF)
    own_dh[...] = d_hidden
    send(own_dh, other_dh, S_SWAP_DH, SWAP_DH, expert=partner).start()

    def send_back(out, into, s, r):
        for k in (2, 1, 3):
            send(out.at[k], into.at[owners - k], s, r, expert=z_peer(k)).start()
        into[0] = out[0]

    send_back(y_out, y_in, S_Y, Y)

    def choose(other, own, dst):
        turned = jnp.concatenate([other[count // 2 :], other[: count // 2]], axis=0)
        dst[0] = jnp.where(flag == 1, turned, own[...])

    def tell(buf, s, r, r_twin):
        for i in (2, 1, 3):
            send(buf.at[0], buf.at[4 - i], s, r + 3 - i, dp=peer(i)).start()
        send(buf.at[0], buf.at[4], s, r_twin, dp=twin).start()

    def retell(buf, s, r, r_twin):
        for i in (1, 2, 3):
            arrived(buf.at[i], r + i - 1)
            send(buf.at[i], buf.at[4 + i], s, r_twin, dp=twin).start()

    arrived(other_act, SWAP_ACT)
    choose(other_act, own_act, act_all)
    tell(act_all, S_ACT, ACT_IN, ACT_TWIN)

    fold(dot(dot(pack, d_hidden, TN).astype(BF), up, NT), dx_out)
    send_back(dx_out, dx_in, S_DX, DX)

    arrived(other_dh, SWAP_DH)
    choose(other_dh, own_dh, dh_all)
    tell(dh_all, S_DH, DH_IN, DH_TWIN)
    retell(act_all, S_ACT, ACT_IN, ACT_TWIN)

    total = groups * count
    others = pl.ds(1, groups - 1)
    arrived(og_in.at[others, 0], OG_OWN)
    arrived(og_in.at[others, rest], OG_REST)
    arrived(act_all.at[pl.ds(4, 4)], ACT_TWIN)
    down_out[...] = (
        dot(act_all[...].reshape(total, fw), og_in[...].reshape(total, part), TN)
        .astype(BF)
        .reshape(groups, depth, part)
    )
    for f in range(1, groups):
        p = peer(f)
        send(down_out.at[p], down_in.at[back(f)], S_DOWN, DOWN, dp=p).start()
    down_in[0] = down_out[group]
    retell(dh_all, S_DH, DH_IN, DH_TWIN)
    arrived(x_in.at[others, 0], X_OWN)
    arrived(x_in.at[others, rest], X_REST)
    arrived(dh_all.at[pl.ds(4, 4)], DH_TWIN)
    ugrad_ref[0] = dot(x_in[...].reshape(total, part), dh_all[...].reshape(total, fw), TN)

    arrived(y_in.at[rest], Y)
    unfold(y_in, out_ref)
    arrived(down_in.at[others], DOWN)
    for f in range(groups):
        dgrad_ref[0, :, cols(peer(f))] = down_in[f].astype(F32)
    arrived(dx_in.at[rest], DX)
    unfold(dx_in, tgrad_ref)

    for buf, s in ((xs, S_X), (ogs, S_OG)):

        @pl.when(middle)
        def _():
            departed(buf, s)

        @pl.when(jnp.logical_not(middle))
        def _():
            departed(buf.at[pl.ds(0, 2)], s)

    departed(x_in.at[others, 0], S_X_OWN)
    departed(og_in.at[others, 0], S_OG_OWN)
    departed(x_in.at[others, rest], S_X_REST)
    departed(og_in.at[others, rest], S_OG_REST)
    departed(own_act, S_SWAP_ACT)
    departed(own_dh, S_SWAP_DH)
    departed(act_all.at[others], S_ACT)
    departed(dh_all.at[others], S_DH)
    departed(down_in.at[others], S_DOWN)
    departed(y_in.at[rest], S_Y)
    departed(dx_in.at[rest], S_DX)


def place(*refs):
    count = (len(refs) - 1) // 2
    copies = [
        pltpu.make_async_copy(refs[i], refs[count + i], refs[-1].at[i]) for i in range(count)
    ]
    for copy in copies:
        copy.start()
    for copy in copies:
        copy.wait()


def by_kernel(groups, owners, tokens, out_grad, gate_weights, expert_ids, swapped, up, down):
    tok, width = tokens.shape
    fw = up.shape[2]
    part, depth, count = width // groups, fw // groups, owners * tok
    vmem = pl.BlockSpec(memory_space=pltpu.VMEM)
    hbm = pl.BlockSpec(memory_space=pltpu.HBM)
    dma = pltpu.SemaphoreType.DMA
    shapes = (
        ((tok, width), BF),
        ((tok, width), BF),
        ((1, part, fw), F32),
        ((1, depth, width), F32),
    )
    cut = pltpu.VMEM((groups, owners, tok, part), BF)
    hid = pltpu.VMEM((count, fw), BF)
    every = pltpu.VMEM((groups, count, fw), BF)
    folded = pltpu.VMEM((owners, tok, width // 2 + width // 8), BF)
    block = pltpu.VMEM((groups, depth, part), BF)
    params = pltpu.CompilerParams(
        collective_id=0, has_side_effects=True, vmem_limit_bytes=62 << 20
    )
    results = pl.pallas_call(
        kernel,
        out_shape=tuple(pltpu.VMEM(*a) for a in shapes),
        in_specs=[pl.BlockSpec(memory_space=pltpu.SMEM), hbm, hbm, vmem, vmem, hbm, hbm],
        out_specs=(vmem,) * 4,
        scratch_shapes=[
            pltpu.VMEM((owners, tok, width + 128), BF),
            pltpu.VMEM((owners, tok, width), BF),
            pltpu.VMEM(up.shape[1:], BF),
            pltpu.VMEM(down.shape[1:], BF),
            cut,
            cut,
            hid,
            hid,
            hid,
            hid,
            every,
            every,
            folded,
            folded,
            folded,
            folded,
            block,
            block,
            dma((4,)),
            dma((DEPARTURES,)),
            dma((ARRIVALS,)),
        ],
        compiler_params=params,
    )(swapped, tokens, out_grad, gate_weights.T, expert_ids.T, up, down)
    return pl.pallas_call(
        place,
        out_shape=tuple(jax.ShapeDtypeStruct(*a) for a in shapes),
        in_specs=[vmem] * 4,
        out_specs=(hbm,) * 4,
        scratch_shapes=[dma((4,))],
        compiler_params=pltpu.CompilerParams(vmem_limit_bytes=40 << 20),
    )(*results)


def solution(mesh):
    groups, owners = mesh.shape["dp"], mesh.shape["expert"]

    def on_device(tokens, out_grad, gate_weights, expert_ids, swapped, up_weight, down_weight):
        args = (tokens, out_grad, gate_weights, expert_ids, swapped, up_weight, down_weight)
        tok, width = tokens.shape
        fw = up_weight.shape[2]
        known = (groups, owners, tok, expert_ids.shape[1]) == (8, 4, 16, 2)
        if known and width % (128 * groups) == 0 and fw % (16 * groups) == 0:
            return by_kernel(groups, owners, *args)
        return by_collectives(*args)

    rows = P(("dp", "expert"), None)
    in_specs = (rows, rows, rows, rows, P(), P("expert", None, None), P("expert", None, None))
    out_specs = (rows, rows, P("expert", "dp", None), P("expert", "dp", None))
    return jax.shard_map(
        on_device, mesh=mesh, in_specs=in_specs, out_specs=out_specs, check_vma=False
    )
```

```python
import functools

import jax
import jax.numpy as jnp
from jax import lax
from jax.experimental import pallas as pl
from jax.experimental.pallas import tpu as pltpu
from jax.sharding import PartitionSpec as P

BF = jnp.bfloat16
F32 = jnp.float32


def by_collectives(tokens, out_grad, gate_weights, expert_ids, swapped, up_weight, down_weight):
    owners = lax.axis_size("expert")
    mine = lax.axis_index("expert")
    width = tokens.shape[1]
    lanes = jnp.arange(128, dtype=jnp.int32)
    hit = expert_ids[:, :, None] == lanes[None, None, :]
    gates = jnp.sum(jnp.where(hit, gate_weights.astype(F32)[:, :, None], 0.0), axis=1).astype(BF)
    packed = jnp.concatenate([tokens, out_grad, gates], axis=1)
    full = lax.all_gather(packed, "expert", axis=0, tiled=True)
    x, og, gates = full[:, :width], full[:, width : 2 * width], full[:, 2 * width :]
    gates = gates.astype(F32)
    flag = lax.dynamic_slice_in_dim(swapped, mine, 1, 0)[0] == 1
    held = jnp.where(flag, (mine + owners // 2) % owners, mine)

    def column(e):
        return jnp.sum(jnp.where(lanes[None, :] == e, gates, 0.0), axis=1, keepdims=True)

    gate = column(mine)
    up, down = up_weight[0], down_weight[0]
    dy = (gate * og.astype(F32)).astype(BF)
    hidden = jnp.dot(x, up, preferred_element_type=F32)
    d_active = lax.dot_general(dy, down, (((1,), (1,)), ((), ())), preferred_element_type=F32)
    sigma = jax.nn.sigmoid(hidden)
    active = jnp.where(gate > 0, hidden * sigma, 0.0).astype(BF)
    d_hidden = (d_active * sigma * (1.0 + hidden * (1.0 - sigma))).astype(BF)
    other = lax.ppermute(
        jnp.concatenate([active, d_hidden], axis=1),
        "expert",
        [(i, (i + owners // 2) % owners) for i in range(owners)],
    )
    y = jnp.dot(active, down, preferred_element_type=F32).astype(BF).astype(F32)
    dx = lax.dot_general(d_hidden, up, (((1,), (1,)), ((), ())), preferred_element_type=F32)
    back = jnp.concatenate([(gate * y).astype(BF), dx.astype(BF)], axis=1)
    back = lax.psum_scatter(back, "expert", scatter_dimension=0, tiled=True)
    fw = active.shape[1]
    act_h = jnp.where(flag, other[:, :fw], active)
    dh_h = jnp.where(flag, other[:, fw:], d_hidden)
    dy_h = (column(held) * og.astype(F32)).astype(BF)
    over = (((0,), (0,)), ((), ()))
    part_up = lax.dot_general(x, dh_h, over, preferred_element_type=F32).astype(BF)
    part_down = lax.dot_general(act_h, dy_h, over, preferred_element_type=F32).astype(BF)
    sum_up = lax.psum_scatter(part_up, "dp", scatter_dimension=0, tiled=True).astype(F32)
    sum_down = lax.psum_scatter(part_down, "dp", scatter_dimension=0, tiled=True).astype(F32)
    return back[:, :width], back[:, width:], sum_up[None], sum_down[None]


NT = (((1,), (1,)), ((), ()))
TN = (((0,), (0,)), ((), ()))


def dot(a, b, dims=(((1,), (0,)), ((), ()))):
    return lax.dot_general(a, b, dims, preferred_element_type=F32)


X_OWN, OG_OWN, X_REST, OG_REST, SWAP_ACT, SWAP_DH = range(6)
ACT_IN, ACT_TWIN, DH_IN, DH_TWIN, DOWN, Y, DX, GATES = 6, 9, 10, 13, 14, 15, 16, 17
X_IN, OG_IN = 18, 21
GATES_ALL = 24
ARRIVALS = 25
S_X, S_OG, S_X_ON, S_OG_ON, S_X_OWN, S_OG_OWN, S_X_REST, S_OG_REST = range(8)
S_SWAP_ACT, S_SWAP_DH, S_ACT, S_DH, S_DOWN, S_Y, S_DX, S_GATES, S_GATES_ALL = range(8, 17)
DEPARTURES = 17


def kernel(
    swapped_hbm,
    tok_ref,
    og_ref,
    gate_hbm,
    ids_hbm,
    up_ref,
    down_ref,
    out_ref,
    tgrad_ref,
    ugrad_ref,
    dgrad_ref,
    xs,
    ogs,
    gs,
    gs_all,
    x_rows,
    og_rows,
    up_buf,
    down_buf,
    x_in,
    og_in,
    own_act,
    own_dh,
    other_act,
    other_dh,
    act_all,
    dh_all,
    y_out,
    y_in,
    dx_out,
    dx_in,
    down_out,
    down_in,
    swapped_ref,
    gate_ref,
    ids_ref,
    load,
    left,
    came,
):
    owners, groups = 4, 8
    tok, width = tok_ref.shape
    fw = up_ref.shape[2]
    part, depth, half, eighth = width // groups, fw // groups, width // 2, width // 8
    count = owners * tok
    room = own_act.shape[0]
    me = lax.axis_index("expert")
    group = lax.axis_index("dp")
    chip, core = group // 2, lax.rem(group, 2)
    middle = jnp.logical_or(me == 1, me == 2)
    twin = 2 * chip + 1 - core

    def peer(f):
        return 2 * lax.rem(chip + f % 4, 4) + lax.rem(core + f // 4, 2)

    def back(f):
        return f // 4 * 4 + (4 - f % 4) % 4

    def cols(p):
        return pl.ds(pl.multiple_of(p * part, 128), part)

    def z_peer(k):
        return lax.rem(me + k, owners)

    def send(src, dst, s, r, **where):
        return pltpu.make_async_remote_copy(
            src_ref=src,
            dst_ref=dst,
            send_sem=left.at[s],
            recv_sem=came.at[r],
            device_id=where,
            device_id_type=pl.DeviceIdType.MESH,
        )

    def arrived(dst, r):
        send(dst, dst, 0, r, dp=twin).wait_recv()

    def departed(src, s):
        send(src, src, s, 0, dp=twin).wait_send()

    barrier = pltpu.get_barrier_semaphore()
    for k in range(1, owners):
        pl.semaphore_signal(
            barrier, inc=1, device_id={"expert": z_peer(k)}, device_id_type=pl.DeviceIdType.MESH
        )
    for f in range(1, groups):
        pl.semaphore_signal(
            barrier, inc=1, device_id={"dp": peer(f)}, device_id_type=pl.DeviceIdType.MESH
        )
    small = [
        pltpu.make_async_copy(ids_hbm, ids_ref, load.at[4]),
        pltpu.make_async_copy(gate_hbm, gate_ref, load.at[5]),
        pltpu.make_async_copy(swapped_hbm, swapped_ref, load.at[6]),
    ]
    for copy in small:
        copy.start()
    loads = [
        pltpu.make_async_copy(tok_ref, xs.at[0], load.at[0]),
        pltpu.make_async_copy(og_ref, ogs.at[0], load.at[1]),
        pltpu.make_async_copy(up_ref.at[0], up_buf, load.at[2]),
        pltpu.make_async_copy(down_ref.at[0], down_buf, load.at[3]),
    ]
    for copy in loads:
        copy.start()
    for copy in small:
        copy.wait()
    lines = lax.broadcasted_iota(jnp.int32, (128, tok), 0)
    dense = jnp.zeros((128, tok), F32)
    for k in range(ids_ref.shape[0]):
        hit = ids_ref[k : k + 1, :] == lines
        dense += jnp.where(hit, gate_ref[k : k + 1, :].astype(F32), 0.0)
    eye = (
        lax.broadcasted_iota(jnp.int32, (128, 128), 0)
        == lax.broadcasted_iota(jnp.int32, (128, 128), 1)
    ).astype(BF)
    own_gates = dot(dense.astype(BF), eye, TN)
    gs[0] = own_gates.astype(BF)

    def column(v, e):
        lane = lax.broadcasted_iota(jnp.int32, v.shape, 1)
        return jnp.sum(jnp.where(lane == e, v, 0.0), axis=1, keepdims=True)

    def before(hits):
        rows = hits.shape[0]
        r = lax.broadcasted_iota(jnp.int32, (rows, rows), 0)
        c = lax.broadcasted_iota(jnp.int32, (rows, rows), 1)
        earlier = jnp.logical_and(c < r, c // tok == r // tok).astype(BF)
        return dot(earlier, hits.astype(BF))

    def named(gates, e, lanes):
        pick = lax.broadcasted_iota(jnp.int32, (128, lanes), 0) == e
        return (dot(gates, pick.astype(BF)) > 0).astype(F32)

    def packing(hits, turn):
        rank = before(hits)
        block = lax.broadcasted_iota(jnp.int32, hits.shape, 0) // tok
        block = ((block + turn) & 3).astype(F32)
        row = jnp.where(rank < 8, 8 * block + rank, 32 + 2 * block + rank - 8)
        lane = lax.broadcasted_iota(jnp.int32, hits.shape, 1).astype(F32)
        return jnp.where(lane == row, hits, 0.0).astype(BF)

    def fold(y, dst):
        for k in range(owners):
            rows = y[8 * k : 8 * k + 8]
            dst[k, :, :half] = jnp.concatenate([rows[:, :half], rows[:, half:]], axis=0).astype(BF)
        rest = jnp.concatenate(
            [y[32:40, eighth * j : eighth * (j + 1)] for j in range(8)], axis=0
        ).astype(BF)
        dst[:, :, half:] = dot(perm, rest).astype(BF).reshape(owners, tok, eighth)

    def unfold(src, dst):
        main = dot(main_pick, src[:, :, :half].reshape(count, half))
        rest = dot(rest_pick, src[:, :, half:].reshape(count, eighth))
        for q in range(8):
            h, at = q // 4, q % 4 * eighth
            dst[:, q * eighth : (q + 1) * eighth] = (
                main[tok * h : tok * (h + 1), at : at + eighth] + rest[tok * q : tok * (q + 1)]
            ).astype(BF)

    flag = swapped_ref[me]
    pl.semaphore_wait(barrier, owners + groups - 2)

    def gather(src, buf, s, r):
        for d, there in ((2, me < 2), (-2, me > 1), (1, me < 3), (-1, me > 0)):
            slot = -d % owners

            @pl.when(there)
            def _():
                send(
                    src, buf.at[slot], s, r + slot - 1, expert=lax.rem(me + d + owners, owners)
                ).start()

    def pass_on(buf, s, r):
        arrived(buf.at[2], r + 1)
        slot = 1 + 2 * lax.rem(me, 2)

        @pl.when(middle)
        def _():
            pltpu.make_async_remote_copy(
                src_ref=buf.at[2],
                dst_ref=buf.at[slot],
                send_sem=left.at[s],
                recv_sem=came.at[r + slot - 1],
                device_id={"expert": lax.rem(3 * (me + 3), owners)},
                device_id_type=pl.DeviceIdType.MESH,
            ).start()

    def spread_own(src, dst, s, r):
        for f in range(1, groups):
            p = peer(f)
            send(src.at[:, cols(p)], dst.at[back(f), 0], s, r, dp=p).start()

    rest = pl.ds(1, owners - 1)

    def spread_rest(buf, dst, s, r):
        for f in range(1, groups):
            p = peer(f)
            send(buf.at[rest, :, cols(p)], dst.at[back(f), rest], s, r, dp=p).start()
        dst[0, 1:] = buf[1:, :, cols(group)]

    for k in (2, 1, 3):
        send(gs.at[0], gs.at[owners - k], S_GATES, GATES, expert=z_peer(k)).start()
    gather(tok_ref, xs, S_X, X_IN)
    gather(og_ref, ogs, S_OG, OG_IN)
    spread_own(tok_ref, x_in, S_X_OWN, X_OWN)
    spread_own(og_ref, og_in, S_OG_OWN, OG_OWN)
    pass_on(xs, S_X_ON, X_IN)
    arrived(xs.at[1], X_IN)
    arrived(xs.at[3], X_IN + 2)
    loads[0].wait()
    x_in[0, 0] = xs[0, :, cols(group)]
    spread_rest(xs, x_in, S_X_REST, X_REST)
    pass_on(ogs, S_OG_ON, OG_IN)

    arrived(gs.at[rest], GATES)
    for f in range(1, groups):
        send(gs, gs_all.at[back(f)], S_GATES_ALL, GATES_ALL, dp=peer(f)).start()
    gs_all[0] = gs[...]
    gates = gs[...].reshape(count, 128)
    gate = column(gates.astype(F32), me)
    pack = packing(named(gates, me, room), 0)

    loads[2].wait()
    up = up_buf[...]
    hidden = dot(xs[...].reshape(count, width), up)
    sigma = 1.0 / (1.0 + jnp.exp(-hidden))
    active = (gate * (hidden * sigma)).astype(BF)
    slope = sigma * (1.0 + hidden * (1.0 - sigma))
    own_act[...] = dot(pack, active, TN).astype(BF)
    partner = lax.rem(me + 2, owners)
    send(own_act, other_act, S_SWAP_ACT, SWAP_ACT, expert=partner).start()
    spot = lax.broadcasted_iota(jnp.int32, (1, count), 1)
    own_hits = named(own_gates.astype(BF), (me + spot // tok) & 3, count)
    own_rank = before(own_hits)
    spot = (spot & (tok - 1)).astype(F32)
    low = jnp.where(own_rank < 8, own_hits, 0.0)
    high = own_hits - low
    main_pick = [jnp.where(spot == 8 * h + own_rank, low, 0.0) for h in range(2)]
    rest_pick = [jnp.where(spot == 2 * q + own_rank - 8, high, 0.0) for q in range(8)]
    main_pick = jnp.concatenate(main_pick, axis=0).astype(BF)
    rest_pick = jnp.concatenate(rest_pick, axis=0).astype(BF)
    c = lax.broadcasted_iota(jnp.int32, (count, count), 1)
    perm = (
        lax.broadcasted_iota(jnp.int32, (count, count), 0)
        == 16 * ((c >> 1) & 3) + 2 * (c >> 3) + (c & 1)
    ).astype(BF)

    loads[3].wait()
    down = down_buf[...]
    fold(dot(own_act[...], down), y_out)

    arrived(ogs.at[1], OG_IN)
    arrived(ogs.at[3], OG_IN + 2)
    loads[1].wait()
    og_in[0, 0] = ogs[0, :, cols(group)]
    spread_rest(ogs, og_in, S_OG_REST, OG_REST)
    dy = (gate * ogs[...].reshape(count, width).astype(F32)).astype(BF)
    d_hidden = (dot(dy, down, NT) * slope).astype(BF)
    own_dh[...] = dot(pack, d_hidden, TN).astype(BF)
    send(own_dh, other_dh, S_SWAP_DH, SWAP_DH, expert=partner).start()

    def send_back(out, into, s, r):
        for k in (2, 1, 3):
            send(out.at[k], into.at[owners - k], s, r, expert=z_peer(k)).start()
        into[0] = out[0]


    def choose(other, own, dst):
        dst[0] = jnp.where(flag == 1, other[...], own[...])

    def tell(buf, s, r, r_twin):
        for i in (2, 1, 3):
            send(buf.at[0], buf.at[4 - i], s, r + 3 - i, dp=peer(i)).start()
        send(buf.at[0], buf.at[4], s, r_twin, dp=twin).start()

    def retell(buf, s, r, r_twin):
        for i in (1, 2, 3):
            arrived(buf.at[i], r + i - 1)
            send(buf.at[i], buf.at[4 + i], s, r_twin, dp=twin).start()

    arrived(other_act, SWAP_ACT)
    choose(other_act, own_act, act_all)
    tell(act_all, S_ACT, ACT_IN, ACT_TWIN)
    send_back(y_out, y_in, S_Y, Y)

    fold(dot(own_dh[...], up, NT), dx_out)

    held = jnp.where(flag == 1, partner, me)
    others = pl.ds(1, groups - 1)
    arrived(gs_all.at[others], GATES_ALL)
    turn = jnp.where(flag == 1, 2, 0)
    hits = named(gs_all[...].reshape(groups * count, 128), held, room)
    packs = [packing(hits[count * f : count * (f + 1)], turn) for f in range(groups)]
    arrived(x_in.at[others, 0], X_OWN)
    arrived(x_in.at[others, rest], X_REST)
    for f in range(groups):
        x_rows[f] = dot(packs[f], x_in[f].reshape(count, part), TN).astype(BF)

    arrived(other_dh, SWAP_DH)
    choose(other_dh, own_dh, dh_all)
    tell(dh_all, S_DH, DH_IN, DH_TWIN)
    send_back(dx_out, dx_in, S_DX, DX)
    retell(act_all, S_ACT, ACT_IN, ACT_TWIN)

    total = groups * room
    arrived(og_in.at[others, 0], OG_OWN)
    arrived(og_in.at[others, rest], OG_REST)
    for f in range(groups):
        og_rows[f] = dot(packs[f], og_in[f].reshape(count, part), TN).astype(BF)
    arrived(act_all.at[pl.ds(4, 4)], ACT_TWIN)
    down_out[...] = (
        dot(act_all[...].reshape(total, fw), og_rows[...].reshape(total, part), TN)
        .astype(BF)
        .reshape(groups, depth, part)
    )
    for f in range(1, groups):
        p = peer(f)
        send(down_out.at[p], down_in.at[back(f)], S_DOWN, DOWN, dp=p).start()
    down_in[0] = down_out[group]
    retell(dh_all, S_DH, DH_IN, DH_TWIN)
    arrived(dh_all.at[pl.ds(4, 4)], DH_TWIN)
    ugrad_ref[0] = dot(x_rows[...].reshape(total, part), dh_all[...].reshape(total, fw), TN)

    arrived(y_in.at[rest], Y)
    unfold(y_in, out_ref)
    arrived(down_in.at[others], DOWN)
    for f in range(groups):
        dgrad_ref[0, :, cols(peer(f))] = down_in[f].astype(F32)
    arrived(dx_in.at[rest], DX)
    unfold(dx_in, tgrad_ref)

    for buf, s, s_on in ((xs, S_X, S_X_ON), (ogs, S_OG, S_OG_ON)):

        @pl.when(middle)
        def _():
            departed(buf.at[rest], s)
            departed(buf.at[0], s_on)

        @pl.when(jnp.logical_not(middle))
        def _():
            departed(buf.at[pl.ds(0, 2)], s)

    departed(gs.at[rest], S_GATES)
    departed(gs_all.at[others], S_GATES_ALL)
    departed(x_in.at[others, 0], S_X_OWN)
    departed(og_in.at[others, 0], S_OG_OWN)
    departed(x_in.at[others, rest], S_X_REST)
    departed(og_in.at[others, rest], S_OG_REST)
    departed(own_act, S_SWAP_ACT)
    departed(own_dh, S_SWAP_DH)
    departed(act_all.at[others], S_ACT)
    departed(dh_all.at[others], S_DH)
    departed(down_in.at[others], S_DOWN)
    departed(y_in.at[rest], S_Y)
    departed(dx_in.at[rest], S_DX)


def place(*refs):
    count = (len(refs) - 1) // 2
    copies = [
        pltpu.make_async_copy(refs[i], refs[count + i], refs[-1].at[i]) for i in range(count)
    ]
    for copy in copies:
        copy.start()
    for copy in copies:
        copy.wait()


def by_kernel(groups, owners, tokens, out_grad, gate_weights, expert_ids, swapped, up, down):
    tok, width = tokens.shape
    fw = up.shape[2]
    part, depth, count = width // groups, fw // groups, owners * tok
    vmem = pl.BlockSpec(memory_space=pltpu.VMEM)
    hbm = pl.BlockSpec(memory_space=pltpu.HBM)
    dma = pltpu.SemaphoreType.DMA
    shapes = (
        ((tok, width), BF),
        ((tok, width), BF),
        ((1, part, fw), F32),
        ((1, depth, width), F32),
    )
    cut = pltpu.VMEM((groups, owners, tok, part), BF)
    room = 48
    hid = pltpu.VMEM((room, fw), BF)
    every = pltpu.VMEM((groups, room, fw), BF)
    folded = pltpu.VMEM((owners, tok, width // 2 + width // 8), BF)
    block = pltpu.VMEM((groups, depth, part), BF)
    params = pltpu.CompilerParams(
        collective_id=0, has_side_effects=True, vmem_limit_bytes=62 << 20
    )
    results = pl.pallas_call(
        kernel,
        out_shape=tuple(pltpu.VMEM(*a) for a in shapes),
        in_specs=[hbm] * 7,
        out_specs=(vmem,) * 4,
        scratch_shapes=[
            pltpu.VMEM((owners, tok, width), BF),
            pltpu.VMEM((owners, tok, width), BF),
            pltpu.VMEM((owners, tok, 128), BF),
            pltpu.VMEM((groups, owners, tok, 128), BF),
            pltpu.VMEM((groups, room, part), BF),
            pltpu.VMEM((groups, room, part), BF),
            pltpu.VMEM(up.shape[1:], BF),
            pltpu.VMEM(down.shape[1:], BF),
            cut,
            cut,
            hid,
            hid,
            hid,
            hid,
            every,
            every,
            folded,
            folded,
            folded,
            folded,
            block,
            block,
            pltpu.SMEM(swapped.shape, swapped.dtype),
            pltpu.VMEM(gate_weights.shape[::-1], BF),
            pltpu.VMEM(expert_ids.shape[::-1], jnp.int32),
            dma((7,)),
            dma((DEPARTURES,)),
            dma((ARRIVALS,)),
        ],
        compiler_params=params,
    )(swapped, tokens, out_grad, gate_weights.T, expert_ids.T, up, down)
    return pl.pallas_call(
        place,
        out_shape=tuple(jax.ShapeDtypeStruct(*a) for a in shapes),
        in_specs=[vmem] * 4,
        out_specs=(hbm,) * 4,
        scratch_shapes=[dma((4,))],
        compiler_params=pltpu.CompilerParams(vmem_limit_bytes=40 << 20),
    )(*results)


def solution(mesh):
    groups, owners = mesh.shape["dp"], mesh.shape["expert"]

    def on_device(tokens, out_grad, gate_weights, expert_ids, swapped, up_weight, down_weight):
        args = (tokens, out_grad, gate_weights, expert_ids, swapped, up_weight, down_weight)
        tok, width = tokens.shape
        fw = up_weight.shape[2]
        known = (groups, owners, tok, expert_ids.shape[1]) == (8, 4, 16, 2)
        if known and width % (128 * groups) == 0 and fw % (16 * groups) == 0:
            return by_kernel(groups, owners, *args)
        return by_collectives(*args)

    rows = P(("dp", "expert"), None)
    in_specs = (rows, rows, rows, rows, P(), P("expert", None, None), P("expert", None, None))
    out_specs = (rows, rows, P("expert", "dp", None), P("expert", "dp", None))
    return jax.shard_map(
        on_device, mesh=mesh, in_specs=in_specs, out_specs=out_specs, check_vma=False
    )
```

```python
import functools

import jax
import jax.numpy as jnp
from jax import lax
from jax.experimental import pallas as pl
from jax.experimental.pallas import tpu as pltpu
from jax.sharding import PartitionSpec as P

BF = jnp.bfloat16
F32 = jnp.float32


def by_collectives(tokens, out_grad, gate_weights, expert_ids, swapped, up_weight, down_weight):
    owners = lax.axis_size("expert")
    mine = lax.axis_index("expert")
    width = tokens.shape[1]
    lanes = jnp.arange(128, dtype=jnp.int32)
    hit = expert_ids[:, :, None] == lanes[None, None, :]
    gates = jnp.sum(jnp.where(hit, gate_weights.astype(F32)[:, :, None], 0.0), axis=1).astype(BF)
    packed = jnp.concatenate([tokens, out_grad, gates], axis=1)
    full = lax.all_gather(packed, "expert", axis=0, tiled=True)
    x, og, gates = full[:, :width], full[:, width : 2 * width], full[:, 2 * width :]
    gates = gates.astype(F32)
    flag = lax.dynamic_slice_in_dim(swapped, mine, 1, 0)[0] == 1
    held = jnp.where(flag, (mine + owners // 2) % owners, mine)

    def column(e):
        return jnp.sum(jnp.where(lanes[None, :] == e, gates, 0.0), axis=1, keepdims=True)

    gate = column(mine)
    up, down = up_weight[0], down_weight[0]
    dy = (gate * og.astype(F32)).astype(BF)
    hidden = jnp.dot(x, up, preferred_element_type=F32)
    d_active = lax.dot_general(dy, down, (((1,), (1,)), ((), ())), preferred_element_type=F32)
    sigma = jax.nn.sigmoid(hidden)
    active = jnp.where(gate > 0, hidden * sigma, 0.0).astype(BF)
    d_hidden = (d_active * sigma * (1.0 + hidden * (1.0 - sigma))).astype(BF)
    other = lax.ppermute(
        jnp.concatenate([active, d_hidden], axis=1),
        "expert",
        [(i, (i + owners // 2) % owners) for i in range(owners)],
    )
    y = jnp.dot(active, down, preferred_element_type=F32).astype(BF).astype(F32)
    dx = lax.dot_general(d_hidden, up, (((1,), (1,)), ((), ())), preferred_element_type=F32)
    back = jnp.concatenate([(gate * y).astype(BF), dx.astype(BF)], axis=1)
    back = lax.psum_scatter(back, "expert", scatter_dimension=0, tiled=True)
    fw = active.shape[1]
    act_h = jnp.where(flag, other[:, :fw], active)
    dh_h = jnp.where(flag, other[:, fw:], d_hidden)
    dy_h = (column(held) * og.astype(F32)).astype(BF)
    over = (((0,), (0,)), ((), ()))
    part_up = lax.dot_general(x, dh_h, over, preferred_element_type=F32).astype(BF)
    part_down = lax.dot_general(act_h, dy_h, over, preferred_element_type=F32).astype(BF)
    sum_up = lax.psum_scatter(part_up, "dp", scatter_dimension=0, tiled=True).astype(F32)
    sum_down = lax.psum_scatter(part_down, "dp", scatter_dimension=0, tiled=True).astype(F32)
    return back[:, :width], back[:, width:], sum_up[None], sum_down[None]


NT = (((1,), (1,)), ((), ()))
TN = (((0,), (0,)), ((), ()))


def dot(a, b, dims=(((1,), (0,)), ((), ()))):
    return lax.dot_general(a, b, dims, preferred_element_type=F32)


X_OWN, OG_OWN, X_REST, OG_REST, SWAP_ACT, SWAP_DH = range(6)
ACT_IN, ACT_TWIN, DH_IN, DH_TWIN, DOWN, Y, DX, GATES = 6, 9, 10, 13, 14, 15, 16, 17
X_IN, OG_IN = 18, 21
GATES_ALL = 24
ARRIVALS = 25
S_X, S_OG, S_X_ON, S_OG_ON, S_X_OWN, S_OG_OWN, S_X_REST, S_OG_REST = range(8)
S_SWAP_ACT, S_SWAP_DH, S_ACT, S_DH, S_DOWN, S_Y, S_DX, S_GATES, S_GATES_ALL = range(8, 17)
DEPARTURES = 17


def kernel(
    swapped_hbm,
    tok_ref,
    og_ref,
    gate_hbm,
    ids_hbm,
    up_ref,
    down_ref,
    out_ref,
    tgrad_ref,
    ugrad_ref,
    dgrad_ref,
    xs,
    ogs,
    gs,
    gs_all,
    x_rows,
    og_rows,
    up_buf,
    down_buf,
    up_turned,
    down_turned,
    x_in,
    og_in,
    own_act,
    own_dh,
    other_act,
    other_dh,
    act_all,
    dh_all,
    y_out,
    y_in,
    dx_out,
    dx_in,
    down_out,
    down_in,
    swapped_ref,
    gate_ref,
    ids_ref,
    load,
    left,
    came,
):
    owners, groups = 4, 8
    tok, width = tok_ref.shape
    fw = up_ref.shape[2]
    part, depth, half, eighth = width // groups, fw // groups, width // 2, width // 8
    count = owners * tok
    room = own_act.shape[0]
    me = lax.axis_index("expert")
    group = lax.axis_index("dp")
    chip, core = group // 2, lax.rem(group, 2)
    middle = jnp.logical_or(me == 1, me == 2)
    twin = 2 * chip + 1 - core

    def peer(f):
        return 2 * lax.rem(chip + f % 4, 4) + lax.rem(core + f // 4, 2)

    def back(f):
        return f // 4 * 4 + (4 - f % 4) % 4

    def cols(p):
        return pl.ds(pl.multiple_of(p * part, 128), part)

    def z_peer(k):
        return lax.rem(me + k, owners)

    def send(src, dst, s, r, **where):
        return pltpu.make_async_remote_copy(
            src_ref=src,
            dst_ref=dst,
            send_sem=left.at[s],
            recv_sem=came.at[r],
            device_id=where,
            device_id_type=pl.DeviceIdType.MESH,
        )

    def arrived(dst, r):
        send(dst, dst, 0, r, dp=twin).wait_recv()

    def departed(src, s):
        send(src, src, s, 0, dp=twin).wait_send()

    barrier = pltpu.get_barrier_semaphore()
    for k in range(1, owners):
        pl.semaphore_signal(
            barrier, inc=1, device_id={"expert": z_peer(k)}, device_id_type=pl.DeviceIdType.MESH
        )
    for f in range(1, groups):
        pl.semaphore_signal(
            barrier, inc=1, device_id={"dp": peer(f)}, device_id_type=pl.DeviceIdType.MESH
        )
    small = [
        pltpu.make_async_copy(ids_hbm, ids_ref, load.at[4]),
        pltpu.make_async_copy(gate_hbm, gate_ref, load.at[5]),
        pltpu.make_async_copy(swapped_hbm, swapped_ref, load.at[6]),
    ]
    for copy in small:
        copy.start()
    loads = [
        pltpu.make_async_copy(tok_ref, xs.at[0], load.at[0]),
        pltpu.make_async_copy(og_ref, ogs.at[0], load.at[1]),
        pltpu.make_async_copy(up_ref.at[0], up_buf, load.at[2]),
        pltpu.make_async_copy(down_ref.at[0], down_buf, load.at[3]),
    ]
    for copy in loads:
        copy.start()
    for copy in small:
        copy.wait()
    lines = lax.broadcasted_iota(jnp.int32, (128, tok), 0)
    dense = jnp.zeros((128, tok), F32)
    for k in range(ids_ref.shape[0]):
        hit = ids_ref[k : k + 1, :] == lines
        dense += jnp.where(hit, gate_ref[k : k + 1, :].astype(F32), 0.0)
    eye = (
        lax.broadcasted_iota(jnp.int32, (128, 128), 0)
        == lax.broadcasted_iota(jnp.int32, (128, 128), 1)
    ).astype(BF)
    own_gates = dot(dense.astype(BF), eye, TN)
    gs[0] = own_gates.astype(BF)

    def column(v, e):
        lane = lax.broadcasted_iota(jnp.int32, v.shape, 1)
        return jnp.sum(jnp.where(lane == e, v, 0.0), axis=1, keepdims=True)

    def before(hits):
        rows = hits.shape[0]
        r = lax.broadcasted_iota(jnp.int32, (rows, rows), 0)
        c = lax.broadcasted_iota(jnp.int32, (rows, rows), 1)
        earlier = jnp.logical_and(c < r, c // tok == r // tok).astype(BF)
        return dot(earlier, hits.astype(BF))

    def named(gates, e, lanes):
        pick = lax.broadcasted_iota(jnp.int32, (128, lanes), 0) == e
        return (dot(gates, pick.astype(BF)) > 0).astype(F32)

    def packing(hits, turn):
        rank = before(hits)
        block = lax.broadcasted_iota(jnp.int32, hits.shape, 0) // tok
        block = ((block + turn) & 3).astype(F32)
        row = jnp.where(rank < 8, 8 * block + rank, 32 + 2 * block + rank - 8)
        lane = lax.broadcasted_iota(jnp.int32, hits.shape, 1).astype(F32)
        return jnp.where(lane == row, hits, 0.0).astype(BF)

    def fold(y, dst):
        for k in range(owners):
            rows = y[8 * k : 8 * k + 8]
            dst[k, :, :half] = jnp.concatenate([rows[:, :half], rows[:, half:]], axis=0).astype(BF)
        rest = jnp.concatenate(
            [y[32:40, eighth * j : eighth * (j + 1)] for j in range(8)], axis=0
        ).astype(BF)
        dst[:, :, half:] = dot(perm, rest).astype(BF).reshape(owners, tok, eighth)

    def unfold(src, dst):
        main = dot(main_pick, src[:, :, :half].reshape(count, half))
        rest = dot(rest_pick, src[:, :, half:].reshape(count, eighth))
        for q in range(8):
            h, at = q // 4, q % 4 * eighth
            dst[:, q * eighth : (q + 1) * eighth] = (
                main[tok * h : tok * (h + 1), at : at + eighth] + rest[tok * q : tok * (q + 1)]
            ).astype(BF)

    flag = swapped_ref[me]
    pl.semaphore_wait(barrier, owners + groups - 2)

    def gather(src, buf, s, r):
        for d, there in ((2, me < 2), (-2, me > 1), (1, me < 3), (-1, me > 0)):
            slot = -d % owners

            @pl.when(there)
            def _():
                send(
                    src, buf.at[slot], s, r + slot - 1, expert=lax.rem(me + d + owners, owners)
                ).start()

    def pass_on(buf, s, r):
        arrived(buf.at[2], r + 1)
        slot = 1 + 2 * lax.rem(me, 2)

        @pl.when(middle)
        def _():
            pltpu.make_async_remote_copy(
                src_ref=buf.at[2],
                dst_ref=buf.at[slot],
                send_sem=left.at[s],
                recv_sem=came.at[r + slot - 1],
                device_id={"expert": lax.rem(3 * (me + 3), owners)},
                device_id_type=pl.DeviceIdType.MESH,
            ).start()

    def spread_own(src, dst, s, r):
        for f in range(1, groups):
            p = peer(f)
            send(src.at[:, cols(p)], dst.at[back(f), 0], s, r, dp=p).start()

    rest = pl.ds(1, owners - 1)

    def spread_rest(buf, dst, s, r):
        for f in range(1, groups):
            p = peer(f)
            send(buf.at[rest, :, cols(p)], dst.at[back(f), rest], s, r, dp=p).start()
        dst[0, 1:] = buf[1:, :, cols(group)]

    for k in (2, 1, 3):
        send(gs.at[0], gs.at[owners - k], S_GATES, GATES, expert=z_peer(k)).start()
    gather(tok_ref, xs, S_X, X_IN)
    gather(og_ref, ogs, S_OG, OG_IN)
    spread_own(tok_ref, x_in, S_X_OWN, X_OWN)
    spread_own(og_ref, og_in, S_OG_OWN, OG_OWN)
    loads[3].wait()
    down_turned[...] = down_buf[...].T
    pass_on(xs, S_X_ON, X_IN)
    arrived(xs.at[1], X_IN)
    arrived(xs.at[3], X_IN + 2)
    loads[0].wait()
    x_in[0, 0] = xs[0, :, cols(group)]
    spread_rest(xs, x_in, S_X_REST, X_REST)
    pass_on(ogs, S_OG_ON, OG_IN)

    arrived(gs.at[rest], GATES)
    for f in range(1, groups):
        send(gs, gs_all.at[back(f)], S_GATES_ALL, GATES_ALL, dp=peer(f)).start()
    gs_all[0] = gs[...]
    gates = gs[...].reshape(count, 128)
    gate = column(gates.astype(F32), me)
    pack = packing(named(gates, me, room), 0)

    loads[2].wait()
    up = up_buf[...]
    hidden = dot(xs[...].reshape(count, width), up)
    sigma = 1.0 / (1.0 + jnp.exp(-hidden))
    active = (gate * (hidden * sigma)).astype(BF)
    slope = sigma * (1.0 + hidden * (1.0 - sigma))
    own_act[...] = dot(pack, active, TN).astype(BF)
    partner = lax.rem(me + 2, owners)
    send(own_act, other_act, S_SWAP_ACT, SWAP_ACT, expert=partner).start()
    spot = lax.broadcasted_iota(jnp.int32, (1, count), 1)
    own_hits = named(own_gates.astype(BF), (me + spot // tok) & 3, count)
    own_rank = before(own_hits)
    spot = (spot & (tok - 1)).astype(F32)
    low = jnp.where(own_rank < 8, own_hits, 0.0)
    high = own_hits - low
    main_pick = [jnp.where(spot == 8 * h + own_rank, low, 0.0) for h in range(2)]
    rest_pick = [jnp.where(spot == 2 * q + own_rank - 8, high, 0.0) for q in range(8)]
    main_pick = jnp.concatenate(main_pick, axis=0).astype(BF)
    rest_pick = jnp.concatenate(rest_pick, axis=0).astype(BF)
    c = lax.broadcasted_iota(jnp.int32, (count, count), 1)
    perm = (
        lax.broadcasted_iota(jnp.int32, (count, count), 0)
        == 16 * ((c >> 1) & 3) + 2 * (c >> 3) + (c & 1)
    ).astype(BF)

    down = down_buf[...]
    fold(dot(own_act[...], down), y_out)

    up_turned[...] = up.T
    arrived(ogs.at[1], OG_IN)
    arrived(ogs.at[3], OG_IN + 2)
    loads[1].wait()
    og_in[0, 0] = ogs[0, :, cols(group)]
    spread_rest(ogs, og_in, S_OG_REST, OG_REST)
    dy = (gate * ogs[...].reshape(count, width).astype(F32)).astype(BF)
    d_hidden = (dot(dy, down_turned[...]) * slope).astype(BF)
    own_dh[...] = dot(pack, d_hidden, TN).astype(BF)
    send(own_dh, other_dh, S_SWAP_DH, SWAP_DH, expert=partner).start()

    def send_back(out, into, s, r):
        for p in (0, 1, 2, 3):
            k = lax.rem(p + owners - me, owners)

            @pl.when(me != p)
            def _():
                send(
                    out.at[k], into.at[lax.rem(me + owners - p, owners)], s, r, expert=p
                ).start()

        into[0] = out[0]


    def choose(other, own, dst):
        dst[0] = jnp.where(flag == 1, other[...], own[...])

    def tell(buf, s, r, r_twin):
        for i in (2, 1, 3):
            send(buf.at[0], buf.at[4 - i], s, r + 3 - i, dp=peer(i)).start()
        send(buf.at[0], buf.at[4], s, r_twin, dp=twin).start()

    def retell(buf, s, r, r_twin):
        for i in (1, 2, 3):
            arrived(buf.at[i], r + i - 1)
            send(buf.at[i], buf.at[4 + i], s, r_twin, dp=twin).start()

    arrived(other_act, SWAP_ACT)
    choose(other_act, own_act, act_all)
    tell(act_all, S_ACT, ACT_IN, ACT_TWIN)
    send_back(y_out, y_in, S_Y, Y)

    fold(dot(own_dh[...], up_turned[...]), dx_out)

    held = jnp.where(flag == 1, partner, me)
    others = pl.ds(1, groups - 1)
    arrived(gs_all.at[others], GATES_ALL)
    turn = jnp.where(flag == 1, 2, 0)
    hits = named(gs_all[...].reshape(groups * count, 128), held, room)
    packs = [packing(hits[count * f : count * (f + 1)], turn) for f in range(groups)]
    arrived(x_in.at[others, 0], X_OWN)
    arrived(x_in.at[others, rest], X_REST)
    for f in range(groups):
        x_rows[f] = dot(packs[f], x_in[f].reshape(count, part), TN).astype(BF)

    arrived(other_dh, SWAP_DH)
    choose(other_dh, own_dh, dh_all)
    tell(dh_all, S_DH, DH_IN, DH_TWIN)
    send_back(dx_out, dx_in, S_DX, DX)
    retell(act_all, S_ACT, ACT_IN, ACT_TWIN)

    total = groups * room
    arrived(og_in.at[others, 0], OG_OWN)
    arrived(og_in.at[others, rest], OG_REST)
    for f in range(groups):
        og_rows[f] = dot(packs[f], og_in[f].reshape(count, part), TN).astype(BF)
    arrived(act_all.at[pl.ds(4, 4)], ACT_TWIN)
    down_out[...] = (
        dot(act_all[...].reshape(total, fw), og_rows[...].reshape(total, part), TN)
        .astype(BF)
        .reshape(groups, depth, part)
    )
    for p in (0, 1, 2, 4, 6, 3, 5, 7):
        b, i = lax.rem(p + core, 2), lax.rem(p // 2 + 4 - chip, 4)

        @pl.when(group != p)
        def _():
            send(down_out.at[p], down_in.at[4 * b + lax.rem(4 - i, 4)], S_DOWN, DOWN, dp=p).start()

    down_in[0] = down_out[group]
    retell(dh_all, S_DH, DH_IN, DH_TWIN)
    arrived(dh_all.at[pl.ds(4, 4)], DH_TWIN)
    ugrad_ref[0] = dot(x_rows[...].reshape(total, part), dh_all[...].reshape(total, fw), TN)

    arrived(y_in.at[rest], Y)
    unfold(y_in, out_ref)
    arrived(down_in.at[others], DOWN)
    for f in range(groups):
        dgrad_ref[0, :, cols(peer(f))] = down_in[f].astype(F32)
    arrived(dx_in.at[rest], DX)
    unfold(dx_in, tgrad_ref)

    for buf, s, s_on in ((xs, S_X, S_X_ON), (ogs, S_OG, S_OG_ON)):

        @pl.when(middle)
        def _():
            departed(buf.at[rest], s)
            departed(buf.at[0], s_on)

        @pl.when(jnp.logical_not(middle))
        def _():
            departed(buf.at[pl.ds(0, 2)], s)

    departed(gs.at[rest], S_GATES)
    departed(gs_all.at[others], S_GATES_ALL)
    departed(x_in.at[others, 0], S_X_OWN)
    departed(og_in.at[others, 0], S_OG_OWN)
    departed(x_in.at[others, rest], S_X_REST)
    departed(og_in.at[others, rest], S_OG_REST)
    departed(own_act, S_SWAP_ACT)
    departed(own_dh, S_SWAP_DH)
    departed(act_all.at[others], S_ACT)
    departed(dh_all.at[others], S_DH)
    departed(down_in.at[others], S_DOWN)
    departed(y_in.at[rest], S_Y)
    departed(dx_in.at[rest], S_DX)


def place(*refs):
    count = (len(refs) - 1) // 2
    copies = []
    for i in range(count):
        for j in range(2):
            rows = refs[i].shape[-2] // 2
            at = (0,) * (len(refs[i].shape) - 2) + (pl.ds(j * rows, rows),)
            copies.append(
                pltpu.make_async_copy(refs[i].at[at], refs[count + i].at[at], refs[-1].at[2 * i + j])
            )
    for copy in copies:
        copy.start()
    for copy in copies:
        copy.wait()


def by_kernel(groups, owners, tokens, out_grad, gate_weights, expert_ids, swapped, up, down):
    tok, width = tokens.shape
    fw = up.shape[2]
    part, depth, count = width // groups, fw // groups, owners * tok
    vmem = pl.BlockSpec(memory_space=pltpu.VMEM)
    hbm = pl.BlockSpec(memory_space=pltpu.HBM)
    dma = pltpu.SemaphoreType.DMA
    shapes = (
        ((tok, width), BF),
        ((tok, width), BF),
        ((1, part, fw), F32),
        ((1, depth, width), F32),
    )
    cut = pltpu.VMEM((groups, owners, tok, part), BF)
    room = 48
    hid = pltpu.VMEM((room, fw), BF)
    every = pltpu.VMEM((groups, room, fw), BF)
    folded = pltpu.VMEM((owners, tok, width // 2 + width // 8), BF)
    block = pltpu.VMEM((groups, depth, part), BF)
    params = pltpu.CompilerParams(
        collective_id=0, has_side_effects=True, vmem_limit_bytes=62 << 20
    )
    results = pl.pallas_call(
        kernel,
        out_shape=tuple(pltpu.VMEM(*a) for a in shapes),
        in_specs=[hbm] * 7,
        out_specs=(vmem,) * 4,
        scratch_shapes=[
            pltpu.VMEM((owners, tok, width), BF),
            pltpu.VMEM((owners, tok, width), BF),
            pltpu.VMEM((owners, tok, 128), BF),
            pltpu.VMEM((groups, owners, tok, 128), BF),
            pltpu.VMEM((groups, room, part), BF),
            pltpu.VMEM((groups, room, part), BF),
            pltpu.VMEM(up.shape[1:], BF),
            pltpu.VMEM(down.shape[1:], BF),
            pltpu.VMEM(up.shape[:0:-1], BF),
            pltpu.VMEM(down.shape[:0:-1], BF),
            cut,
            cut,
            hid,
            hid,
            hid,
            hid,
            every,
            every,
            folded,
            folded,
            folded,
            folded,
            block,
            block,
            pltpu.SMEM(swapped.shape, swapped.dtype),
            pltpu.VMEM(gate_weights.shape[::-1], BF),
            pltpu.VMEM(expert_ids.shape[::-1], jnp.int32),
            dma((7,)),
            dma((DEPARTURES,)),
            dma((ARRIVALS,)),
        ],
        compiler_params=params,
    )(swapped, tokens, out_grad, gate_weights.T, expert_ids.T, up, down)
    return pl.pallas_call(
        place,
        out_shape=tuple(jax.ShapeDtypeStruct(*a) for a in shapes),
        in_specs=[vmem] * 4,
        out_specs=(hbm,) * 4,
        scratch_shapes=[dma((8,))],
        compiler_params=pltpu.CompilerParams(vmem_limit_bytes=40 << 20),
    )(*results)


def solution(mesh):
    groups, owners = mesh.shape["dp"], mesh.shape["expert"]

    def on_device(tokens, out_grad, gate_weights, expert_ids, swapped, up_weight, down_weight):
        args = (tokens, out_grad, gate_weights, expert_ids, swapped, up_weight, down_weight)
        tok, width = tokens.shape
        fw = up_weight.shape[2]
        known = (groups, owners, tok, expert_ids.shape[1]) == (8, 4, 16, 2)
        if known and width % (128 * groups) == 0 and fw % (16 * groups) == 0:
            return by_kernel(groups, owners, *args)
        return by_collectives(*args)

    rows = P(("dp", "expert"), None)
    in_specs = (rows, rows, rows, rows, P(), P("expert", None, None), P("expert", None, None))
    out_specs = (rows, rows, P("expert", "dp", None), P("expert", "dp", None))
    return jax.shard_map(
        on_device, mesh=mesh, in_specs=in_specs, out_specs=out_specs, check_vma=False
    )
```

```python
import functools

import jax
import jax.numpy as jnp
from jax import lax
from jax.experimental import pallas as pl
from jax.experimental.pallas import tpu as pltpu
from jax.sharding import PartitionSpec as P

BF = jnp.bfloat16
F32 = jnp.float32


def by_collectives(tokens, out_grad, gate_weights, expert_ids, swapped, up_weight, down_weight):
    owners = lax.axis_size("expert")
    mine = lax.axis_index("expert")
    width = tokens.shape[1]
    lanes = jnp.arange(128, dtype=jnp.int32)
    hit = expert_ids[:, :, None] == lanes[None, None, :]
    gates = jnp.sum(jnp.where(hit, gate_weights.astype(F32)[:, :, None], 0.0), axis=1).astype(BF)
    packed = jnp.concatenate([tokens, out_grad, gates], axis=1)
    full = lax.all_gather(packed, "expert", axis=0, tiled=True)
    x, og, gates = full[:, :width], full[:, width : 2 * width], full[:, 2 * width :]
    gates = gates.astype(F32)
    flag = lax.dynamic_slice_in_dim(swapped, mine, 1, 0)[0] == 1
    held = jnp.where(flag, (mine + owners // 2) % owners, mine)

    def column(e):
        return jnp.sum(jnp.where(lanes[None, :] == e, gates, 0.0), axis=1, keepdims=True)

    gate = column(mine)
    up, down = up_weight[0], down_weight[0]
    dy = (gate * og.astype(F32)).astype(BF)
    hidden = jnp.dot(x, up, preferred_element_type=F32)
    d_active = lax.dot_general(dy, down, (((1,), (1,)), ((), ())), preferred_element_type=F32)
    sigma = jax.nn.sigmoid(hidden)
    active = jnp.where(gate > 0, hidden * sigma, 0.0).astype(BF)
    d_hidden = (d_active * sigma * (1.0 + hidden * (1.0 - sigma))).astype(BF)
    other = lax.ppermute(
        jnp.concatenate([active, d_hidden], axis=1),
        "expert",
        [(i, (i + owners // 2) % owners) for i in range(owners)],
    )
    y = jnp.dot(active, down, preferred_element_type=F32).astype(BF).astype(F32)
    dx = lax.dot_general(d_hidden, up, (((1,), (1,)), ((), ())), preferred_element_type=F32)
    back = jnp.concatenate([(gate * y).astype(BF), dx.astype(BF)], axis=1)
    back = lax.psum_scatter(back, "expert", scatter_dimension=0, tiled=True)
    fw = active.shape[1]
    act_h = jnp.where(flag, other[:, :fw], active)
    dh_h = jnp.where(flag, other[:, fw:], d_hidden)
    dy_h = (column(held) * og.astype(F32)).astype(BF)
    over = (((0,), (0,)), ((), ()))
    part_up = lax.dot_general(x, dh_h, over, preferred_element_type=F32).astype(BF)
    part_down = lax.dot_general(act_h, dy_h, over, preferred_element_type=F32).astype(BF)
    sum_up = lax.psum_scatter(part_up, "dp", scatter_dimension=0, tiled=True).astype(F32)
    sum_down = lax.psum_scatter(part_down, "dp", scatter_dimension=0, tiled=True).astype(F32)
    return back[:, :width], back[:, width:], sum_up[None], sum_down[None]


NT = (((1,), (1,)), ((), ()))
TN = (((0,), (0,)), ((), ()))


def dot(a, b, dims=(((1,), (0,)), ((), ()))):
    return lax.dot_general(a, b, dims, preferred_element_type=F32)


X_OWN, OG_OWN, X_REST, OG_REST, SWAP_ACT, SWAP_DH = range(6)
ACT_IN, ACT_TWIN, DH_IN, DH_TWIN, DOWN, Y, DX, GATES = 6, 9, 10, 13, 14, 15, 16, 17
X_IN, OG_IN = 18, 21
GATES_ALL = 24
ARRIVALS = 25
S_X, S_OG, S_X_ON, S_OG_ON, S_X_OWN, S_OG_OWN, S_X_REST, S_OG_REST = range(8)
S_SWAP_ACT, S_SWAP_DH, S_ACT, S_DH, S_DOWN, S_Y, S_DX, S_GATES, S_GATES_ALL = range(8, 17)
DEPARTURES = 17


def kernel(
    swapped_hbm,
    tok_ref,
    og_ref,
    gate_hbm,
    ids_hbm,
    up_ref,
    down_ref,
    out_ref,
    tgrad_ref,
    ugrad_ref,
    dgrad_ref,
    xs,
    ogs,
    gs,
    gs_all,
    x_rows,
    og_rows,
    up_buf,
    down_buf,
    up_turned,
    down_turned,
    x_in,
    og_in,
    own_act,
    own_dh,
    other_act,
    other_dh,
    act_all,
    dh_all,
    y_out,
    y_in,
    dx_out,
    dx_in,
    down_out,
    down_in,
    swapped_ref,
    gate_ref,
    ids_ref,
    load,
    left,
    came,
):
    owners, groups = 4, 8
    tok, width = tok_ref.shape
    fw = up_ref.shape[2]
    part, depth, half, eighth = width // groups, fw // groups, width // 2, width // 8
    count = owners * tok
    room = own_act.shape[0]
    me = lax.axis_index("expert")
    group = lax.axis_index("dp")
    chip, core = group // 2, lax.rem(group, 2)
    middle = jnp.logical_or(me == 1, me == 2)
    twin = 2 * chip + 1 - core

    def peer(f):
        return 2 * lax.rem(chip + f % 4, 4) + lax.rem(core + f // 4, 2)

    def back(f):
        return f // 4 * 4 + (4 - f % 4) % 4

    def cols(p):
        return pl.ds(pl.multiple_of(p * part, 128), part)

    def z_peer(k):
        return lax.rem(me + k, owners)

    def send(src, dst, s, r, **where):
        return pltpu.make_async_remote_copy(
            src_ref=src,
            dst_ref=dst,
            send_sem=left.at[s],
            recv_sem=came.at[r],
            device_id=where,
            device_id_type=pl.DeviceIdType.MESH,
        )

    def arrived(dst, r):
        send(dst, dst, 0, r, dp=twin).wait_recv()

    def departed(src, s):
        send(src, src, s, 0, dp=twin).wait_send()

    barrier = pltpu.get_barrier_semaphore()
    for k in range(1, owners):
        pl.semaphore_signal(
            barrier, inc=1, device_id={"expert": z_peer(k)}, device_id_type=pl.DeviceIdType.MESH
        )
    for f in range(1, groups):
        pl.semaphore_signal(
            barrier, inc=1, device_id={"dp": peer(f)}, device_id_type=pl.DeviceIdType.MESH
        )
    small = [
        pltpu.make_async_copy(ids_hbm, ids_ref, load.at[4]),
        pltpu.make_async_copy(gate_hbm, gate_ref, load.at[5]),
        pltpu.make_async_copy(swapped_hbm, swapped_ref, load.at[6]),
    ]
    for copy in small:
        copy.start()
    loads = [
        pltpu.make_async_copy(tok_ref, xs.at[0], load.at[0]),
        pltpu.make_async_copy(og_ref, ogs.at[0], load.at[1]),
        pltpu.make_async_copy(up_ref.at[0], up_buf, load.at[2]),
        pltpu.make_async_copy(down_ref.at[0], down_buf, load.at[3]),
    ]
    for copy in loads:
        copy.start()
    for copy in small:
        copy.wait()
    lines = lax.broadcasted_iota(jnp.int32, (128, tok), 0)
    dense = jnp.zeros((128, tok), F32)
    for k in range(ids_ref.shape[0]):
        hit = ids_ref[k : k + 1, :] == lines
        dense += jnp.where(hit, gate_ref[k : k + 1, :].astype(F32), 0.0)
    eye = (
        lax.broadcasted_iota(jnp.int32, (128, 128), 0)
        == lax.broadcasted_iota(jnp.int32, (128, 128), 1)
    ).astype(BF)
    own_gates = dot(dense.astype(BF), eye, TN)
    gs[0] = own_gates.astype(BF)

    def column(v, e):
        lane = lax.broadcasted_iota(jnp.int32, v.shape, 1)
        return jnp.sum(jnp.where(lane == e, v, 0.0), axis=1, keepdims=True)

    def before(hits):
        rows = hits.shape[0]
        r = lax.broadcasted_iota(jnp.int32, (rows, rows), 0)
        c = lax.broadcasted_iota(jnp.int32, (rows, rows), 1)
        earlier = jnp.logical_and(c < r, c // tok == r // tok).astype(BF)
        return dot(earlier, hits.astype(BF))

    def named(gates, e, lanes):
        pick = lax.broadcasted_iota(jnp.int32, (128, lanes), 0) == e
        return (dot(gates, pick.astype(BF)) > 0).astype(F32)

    def packing(hits, turn):
        rank = before(hits)
        block = lax.broadcasted_iota(jnp.int32, hits.shape, 0) // tok
        block = ((block + turn) & 3).astype(F32)
        row = jnp.where(rank < 8, 8 * block + rank, 32 + 2 * block + rank - 8)
        lane = lax.broadcasted_iota(jnp.int32, hits.shape, 1).astype(F32)
        return jnp.where(lane == row, hits, 0.0).astype(BF)

    def fold(y, dst):
        for k in range(owners):
            rows = y[8 * k : 8 * k + 8]
            dst[k, :, :half] = jnp.concatenate([rows[:, :half], rows[:, half:]], axis=0).astype(BF)
        rest = jnp.concatenate(
            [y[32:40, eighth * j : eighth * (j + 1)] for j in range(8)], axis=0
        ).astype(BF)
        dst[:, :, half:] = dot(perm, rest).astype(BF).reshape(owners, tok, eighth)

    def unfold(src, dst):
        main = dot(main_pick, src[:, :, :half].reshape(count, half))
        rest = dot(rest_pick, src[:, :, half:].reshape(count, eighth))
        for q in range(8):
            h, at = q // 4, q % 4 * eighth
            dst[:, q * eighth : (q + 1) * eighth] = (
                main[tok * h : tok * (h + 1), at : at + eighth] + rest[tok * q : tok * (q + 1)]
            ).astype(BF)

    flag = swapped_ref[me]
    pl.semaphore_wait(barrier, owners + groups - 2)

    def gather(src, buf, s, r):
        for d, there in ((2, me < 2), (-2, me > 1), (1, me < 3), (-1, me > 0)):
            slot = -d % owners

            @pl.when(there)
            def _():
                send(
                    src, buf.at[slot], s, r + slot - 1, expert=lax.rem(me + d + owners, owners)
                ).start()

    def pass_on(buf, s, r):
        arrived(buf.at[2], r + 1)
        slot = 1 + 2 * lax.rem(me, 2)

        @pl.when(middle)
        def _():
            pltpu.make_async_remote_copy(
                src_ref=buf.at[2],
                dst_ref=buf.at[slot],
                send_sem=left.at[s],
                recv_sem=came.at[r + slot - 1],
                device_id={"expert": lax.rem(3 * (me + 3), owners)},
                device_id_type=pl.DeviceIdType.MESH,
            ).start()

    def spread_own(src, dst, s, r):
        for f in range(1, groups):
            p = peer(f)
            send(src.at[:, cols(p)], dst.at[back(f), 0], s, r, dp=p).start()

    rest = pl.ds(1, owners - 1)

    def spread_rest(buf, dst, s, r):
        for f in range(1, groups):
            p = peer(f)
            send(buf.at[rest, :, cols(p)], dst.at[back(f), rest], s, r, dp=p).start()
        dst[0, 1:] = buf[1:, :, cols(group)]

    for k in (2, 1, 3):
        send(gs.at[0], gs.at[owners - k], S_GATES, GATES, expert=z_peer(k)).start()
    gather(tok_ref, xs, S_X, X_IN)
    gather(og_ref, ogs, S_OG, OG_IN)
    spread_own(tok_ref, x_in, S_X_OWN, X_OWN)
    spread_own(og_ref, og_in, S_OG_OWN, OG_OWN)
    loads[3].wait()
    down_turned[...] = down_buf[...].T
    pass_on(xs, S_X_ON, X_IN)
    arrived(xs.at[1], X_IN)
    arrived(xs.at[3], X_IN + 2)
    loads[0].wait()
    x_in[0, 0] = xs[0, :, cols(group)]
    spread_rest(xs, x_in, S_X_REST, X_REST)
    pass_on(ogs, S_OG_ON, OG_IN)

    arrived(gs.at[rest], GATES)
    for f in range(1, groups):
        send(gs, gs_all.at[back(f)], S_GATES_ALL, GATES_ALL, dp=peer(f)).start()
    gs_all[0] = gs[...]
    gates = gs[...].reshape(count, 128)
    gate = column(gates.astype(F32), me)
    pack = packing(named(gates, me, room), 0)

    loads[2].wait()
    up = up_buf[...]
    hidden = dot(xs[...].reshape(count, width), up)
    sigma = 1.0 / (1.0 + jnp.exp(-hidden))
    active = (gate * (hidden * sigma)).astype(BF)
    slope = sigma * (1.0 + hidden * (1.0 - sigma))
    own_act[...] = dot(pack, active, TN).astype(BF)
    partner = lax.rem(me + 2, owners)
    send(own_act, other_act, S_SWAP_ACT, SWAP_ACT, expert=partner).start()
    spot = lax.broadcasted_iota(jnp.int32, (1, count), 1)
    own_hits = named(own_gates.astype(BF), (me + spot // tok) & 3, count)
    own_rank = before(own_hits)
    spot = (spot & (tok - 1)).astype(F32)
    low = jnp.where(own_rank < 8, own_hits, 0.0)
    high = own_hits - low
    main_pick = [jnp.where(spot == 8 * h + own_rank, low, 0.0) for h in range(2)]
    rest_pick = [jnp.where(spot == 2 * q + own_rank - 8, high, 0.0) for q in range(8)]
    main_pick = jnp.concatenate(main_pick, axis=0).astype(BF)
    rest_pick = jnp.concatenate(rest_pick, axis=0).astype(BF)
    c = lax.broadcasted_iota(jnp.int32, (count, count), 1)
    perm = (
        lax.broadcasted_iota(jnp.int32, (count, count), 0)
        == 16 * ((c >> 1) & 3) + 2 * (c >> 3) + (c & 1)
    ).astype(BF)

    down = down_buf[...]
    fold(dot(own_act[...], down), y_out)

    up_turned[...] = up.T
    arrived(ogs.at[1], OG_IN)
    arrived(ogs.at[3], OG_IN + 2)
    loads[1].wait()
    og_in[0, 0] = ogs[0, :, cols(group)]
    spread_rest(ogs, og_in, S_OG_REST, OG_REST)
    dy = (gate * ogs[...].reshape(count, width).astype(F32)).astype(BF)
    d_hidden = (dot(dy, down_turned[...]) * slope).astype(BF)
    own_dh[...] = dot(pack, d_hidden, TN).astype(BF)
    send(own_dh, other_dh, S_SWAP_DH, SWAP_DH, expert=partner).start()

    def send_back(out, into, s, r):
        for p in (0, 1, 2, 3):
            k = lax.rem(p + owners - me, owners)

            @pl.when(me != p)
            def _():
                send(
                    out.at[k], into.at[lax.rem(me + owners - p, owners)], s, r, expert=p
                ).start()

        into[0] = out[0]


    def choose(other, own, dst):
        dst[0] = jnp.where(flag == 1, other[...], own[...])

    def tell(buf, s, r, r_twin):
        for to in range(4):
            slot = lax.rem(chip + 4 - to, 4)

            @pl.when(chip != to)
            def _():
                at = lax.rem(slot + 3, 4)
                send(buf.at[0], buf.at[slot], s, r + at, dp=2 * to + core).start()

        send(buf.at[0], buf.at[4], s, r_twin, dp=twin).start()

    def retell(buf, s, r, r_twin):
        for i in (1, 2, 3):
            arrived(buf.at[i], r + i - 1)
            send(buf.at[i], buf.at[4 + i], s, r_twin, dp=twin).start()

    arrived(other_act, SWAP_ACT)
    choose(other_act, own_act, act_all)
    tell(act_all, S_ACT, ACT_IN, ACT_TWIN)
    send_back(y_out, y_in, S_Y, Y)

    fold(dot(own_dh[...], up_turned[...]), dx_out)

    held = jnp.where(flag == 1, partner, me)
    others = pl.ds(1, groups - 1)
    arrived(gs_all.at[others], GATES_ALL)
    turn = jnp.where(flag == 1, 2, 0)
    hits = named(gs_all[...].reshape(groups * count, 128), held, room)
    packs = [packing(hits[count * f : count * (f + 1)], turn) for f in range(groups)]
    arrived(x_in.at[others, 0], X_OWN)
    arrived(x_in.at[others, rest], X_REST)
    for f in range(groups):
        x_rows[f] = dot(packs[f], x_in[f].reshape(count, part), TN).astype(BF)

    arrived(other_dh, SWAP_DH)
    choose(other_dh, own_dh, dh_all)
    tell(dh_all, S_DH, DH_IN, DH_TWIN)
    send_back(dx_out, dx_in, S_DX, DX)
    retell(act_all, S_ACT, ACT_IN, ACT_TWIN)

    total = groups * room
    arrived(og_in.at[others, 0], OG_OWN)
    arrived(og_in.at[others, rest], OG_REST)
    for f in range(groups):
        og_rows[f] = dot(packs[f], og_in[f].reshape(count, part), TN).astype(BF)
    arrived(act_all.at[pl.ds(4, 4)], ACT_TWIN)
    down_out[...] = (
        dot(act_all[...].reshape(total, fw), og_rows[...].reshape(total, part), TN)
        .astype(BF)
        .reshape(groups, depth, part)
    )
    for p in (0, 1, 6, 4, 2, 7, 5, 3):
        b, i = lax.rem(p + core, 2), lax.rem(p // 2 + 4 - chip, 4)

        @pl.when(group != p)
        def _():
            send(down_out.at[p], down_in.at[4 * b + lax.rem(4 - i, 4)], S_DOWN, DOWN, dp=p).start()

    down_in[0] = down_out[group]
    retell(dh_all, S_DH, DH_IN, DH_TWIN)
    arrived(dh_all.at[pl.ds(4, 4)], DH_TWIN)
    ugrad_ref[0] = dot(x_rows[...].reshape(total, part), dh_all[...].reshape(total, fw), TN)

    arrived(y_in.at[rest], Y)
    unfold(y_in, out_ref)
    arrived(down_in.at[others], DOWN)
    for f in range(groups):
        dgrad_ref[0, :, cols(peer(f))] = down_in[f].astype(F32)
    arrived(dx_in.at[rest], DX)
    unfold(dx_in, tgrad_ref)

    for buf, s, s_on in ((xs, S_X, S_X_ON), (ogs, S_OG, S_OG_ON)):

        @pl.when(middle)
        def _():
            departed(buf.at[rest], s)
            departed(buf.at[0], s_on)

        @pl.when(jnp.logical_not(middle))
        def _():
            departed(buf.at[pl.ds(0, 2)], s)

    departed(gs.at[rest], S_GATES)
    departed(gs_all.at[others], S_GATES_ALL)
    departed(x_in.at[others, 0], S_X_OWN)
    departed(og_in.at[others, 0], S_OG_OWN)
    departed(x_in.at[others, rest], S_X_REST)
    departed(og_in.at[others, rest], S_OG_REST)
    departed(own_act, S_SWAP_ACT)
    departed(own_dh, S_SWAP_DH)
    departed(act_all.at[others], S_ACT)
    departed(dh_all.at[others], S_DH)
    departed(down_in.at[others], S_DOWN)
    departed(y_in.at[rest], S_Y)
    departed(dx_in.at[rest], S_DX)


def place(*refs):
    count = (len(refs) - 1) // 2
    copies = []
    for i in range(count):
        for j in range(2):
            rows = refs[i].shape[-2] // 2
            at = (0,) * (len(refs[i].shape) - 2) + (pl.ds(j * rows, rows),)
            copies.append(
                pltpu.make_async_copy(refs[i].at[at], refs[count + i].at[at], refs[-1].at[2 * i + j])
            )
    for copy in copies:
        copy.start()
    for copy in copies:
        copy.wait()


def by_kernel(groups, owners, tokens, out_grad, gate_weights, expert_ids, swapped, up, down):
    tok, width = tokens.shape
    fw = up.shape[2]
    part, depth, count = width // groups, fw // groups, owners * tok
    vmem = pl.BlockSpec(memory_space=pltpu.VMEM)
    hbm = pl.BlockSpec(memory_space=pltpu.HBM)
    dma = pltpu.SemaphoreType.DMA
    shapes = (
        ((tok, width), BF),
        ((tok, width), BF),
        ((1, part, fw), F32),
        ((1, depth, width), F32),
    )
    cut = pltpu.VMEM((groups, owners, tok, part), BF)
    room = 48
    hid = pltpu.VMEM((room, fw), BF)
    every = pltpu.VMEM((groups, room, fw), BF)
    folded = pltpu.VMEM((owners, tok, width // 2 + width // 8), BF)
    block = pltpu.VMEM((groups, depth, part), BF)
    params = pltpu.CompilerParams(
        collective_id=0, has_side_effects=True, vmem_limit_bytes=62 << 20
    )
    results = pl.pallas_call(
        kernel,
        out_shape=tuple(pltpu.VMEM(*a) for a in shapes),
        in_specs=[hbm] * 7,
        out_specs=(vmem,) * 4,
        scratch_shapes=[
            pltpu.VMEM((owners, tok, width), BF),
            pltpu.VMEM((owners, tok, width), BF),
            pltpu.VMEM((owners, tok, 128), BF),
            pltpu.VMEM((groups, owners, tok, 128), BF),
            pltpu.VMEM((groups, room, part), BF),
            pltpu.VMEM((groups, room, part), BF),
            pltpu.VMEM(up.shape[1:], BF),
            pltpu.VMEM(down.shape[1:], BF),
            pltpu.VMEM(up.shape[:0:-1], BF),
            pltpu.VMEM(down.shape[:0:-1], BF),
            cut,
            cut,
            hid,
            hid,
            hid,
            hid,
            every,
            every,
            folded,
            folded,
            folded,
            folded,
            block,
            block,
            pltpu.SMEM(swapped.shape, swapped.dtype),
            pltpu.VMEM(gate_weights.shape[::-1], BF),
            pltpu.VMEM(expert_ids.shape[::-1], jnp.int32),
            dma((7,)),
            dma((DEPARTURES,)),
            dma((ARRIVALS,)),
        ],
        compiler_params=params,
    )(swapped, tokens, out_grad, gate_weights.T, expert_ids.T, up, down)
    return pl.pallas_call(
        place,
        out_shape=tuple(jax.ShapeDtypeStruct(*a) for a in shapes),
        in_specs=[vmem] * 4,
        out_specs=(hbm,) * 4,
        scratch_shapes=[dma((8,))],
        compiler_params=pltpu.CompilerParams(vmem_limit_bytes=40 << 20),
    )(*results)


def solution(mesh):
    groups, owners = mesh.shape["dp"], mesh.shape["expert"]

    def on_device(tokens, out_grad, gate_weights, expert_ids, swapped, up_weight, down_weight):
        args = (tokens, out_grad, gate_weights, expert_ids, swapped, up_weight, down_weight)
        tok, width = tokens.shape
        fw = up_weight.shape[2]
        known = (groups, owners, tok, expert_ids.shape[1]) == (8, 4, 16, 2)
        if known and width % (128 * groups) == 0 and fw % (16 * groups) == 0:
            return by_kernel(groups, owners, *args)
        return by_collectives(*args)

    rows = P(("dp", "expert"), None)
    in_specs = (rows, rows, rows, rows, P(), P("expert", None, None), P("expert", None, None))
    out_specs = (rows, rows, P("expert", "dp", None), P("expert", "dp", None))
    return jax.shard_map(
        on_device, mesh=mesh, in_specs=in_specs, out_specs=out_specs, check_vma=False
    )
```

```python
import functools

import jax
import jax.numpy as jnp
from jax import lax
from jax.experimental import pallas as pl
from jax.experimental.pallas import tpu as pltpu
from jax.sharding import PartitionSpec as P

BF = jnp.bfloat16
F32 = jnp.float32


def by_collectives(tokens, out_grad, gate_weights, expert_ids, swapped, up_weight, down_weight):
    owners = lax.axis_size("expert")
    mine = lax.axis_index("expert")
    width = tokens.shape[1]
    lanes = jnp.arange(128, dtype=jnp.int32)
    hit = expert_ids[:, :, None] == lanes[None, None, :]
    gates = jnp.sum(jnp.where(hit, gate_weights.astype(F32)[:, :, None], 0.0), axis=1).astype(BF)
    packed = jnp.concatenate([tokens, out_grad, gates], axis=1)
    full = lax.all_gather(packed, "expert", axis=0, tiled=True)
    x, og, gates = full[:, :width], full[:, width : 2 * width], full[:, 2 * width :]
    gates = gates.astype(F32)
    flag = lax.dynamic_slice_in_dim(swapped, mine, 1, 0)[0] == 1
    held = jnp.where(flag, (mine + owners // 2) % owners, mine)

    def column(e):
        return jnp.sum(jnp.where(lanes[None, :] == e, gates, 0.0), axis=1, keepdims=True)

    gate = column(mine)
    up, down = up_weight[0], down_weight[0]
    dy = (gate * og.astype(F32)).astype(BF)
    hidden = jnp.dot(x, up, preferred_element_type=F32)
    d_active = lax.dot_general(dy, down, (((1,), (1,)), ((), ())), preferred_element_type=F32)
    sigma = jax.nn.sigmoid(hidden)
    active = jnp.where(gate > 0, hidden * sigma, 0.0).astype(BF)
    d_hidden = (d_active * sigma * (1.0 + hidden * (1.0 - sigma))).astype(BF)
    other = lax.ppermute(
        jnp.concatenate([active, d_hidden], axis=1),
        "expert",
        [(i, (i + owners // 2) % owners) for i in range(owners)],
    )
    y = jnp.dot(active, down, preferred_element_type=F32).astype(BF).astype(F32)
    dx = lax.dot_general(d_hidden, up, (((1,), (1,)), ((), ())), preferred_element_type=F32)
    back = jnp.concatenate([(gate * y).astype(BF), dx.astype(BF)], axis=1)
    back = lax.psum_scatter(back, "expert", scatter_dimension=0, tiled=True)
    fw = active.shape[1]
    act_h = jnp.where(flag, other[:, :fw], active)
    dh_h = jnp.where(flag, other[:, fw:], d_hidden)
    dy_h = (column(held) * og.astype(F32)).astype(BF)
    over = (((0,), (0,)), ((), ()))
    part_up = lax.dot_general(x, dh_h, over, preferred_element_type=F32).astype(BF)
    part_down = lax.dot_general(act_h, dy_h, over, preferred_element_type=F32).astype(BF)
    sum_up = lax.psum_scatter(part_up, "dp", scatter_dimension=0, tiled=True).astype(F32)
    sum_down = lax.psum_scatter(part_down, "dp", scatter_dimension=0, tiled=True).astype(F32)
    return back[:, :width], back[:, width:], sum_up[None], sum_down[None]


NT = (((1,), (1,)), ((), ()))
TN = (((0,), (0,)), ((), ()))


def dot(a, b, dims=(((1,), (0,)), ((), ()))):
    return lax.dot_general(a, b, dims, preferred_element_type=F32)


X_OWN, OG_OWN, X_REST, OG_REST, SWAP_ACT, SWAP_DH = range(6)
ACT_IN, ACT_TWIN, DH_IN, DH_TWIN, DOWN, Y, DX, GATES = 6, 9, 10, 13, 14, 15, 16, 17
X_IN, OG_IN = 18, 21
GATES_ALL = 24
ARRIVALS = 25
S_X, S_OG, S_X_ON, S_OG_ON, S_X_OWN, S_OG_OWN, S_X_REST, S_OG_REST = range(8)
S_SWAP_ACT, S_SWAP_DH, S_ACT, S_DH, S_DOWN, S_Y, S_DX, S_GATES, S_GATES_ALL = range(8, 17)
DEPARTURES = 17


def kernel(
    swapped_hbm,
    tok_ref,
    og_ref,
    gate_hbm,
    ids_hbm,
    up_ref,
    down_ref,
    out_ref,
    tgrad_ref,
    ugrad_ref,
    dgrad_ref,
    xs,
    ogs,
    gs,
    gs_all,
    x_rows,
    og_rows,
    up_buf,
    down_buf,
    up_turned,
    down_turned,
    x_in,
    og_in,
    own_act,
    own_dh,
    other_act,
    other_dh,
    act_all,
    dh_all,
    y_out,
    y_in,
    dx_out,
    dx_in,
    down_out,
    down_in,
    swapped_ref,
    gate_ref,
    ids_ref,
    load,
    left,
    came,
):
    owners, groups = 4, 8
    tok, width = tok_ref.shape
    fw = up_ref.shape[2]
    part, depth, half, eighth = width // groups, fw // groups, width // 2, width // 8
    count = owners * tok
    room = own_act.shape[0]
    me = lax.axis_index("expert")
    group = lax.axis_index("dp")
    chip, core = group // 2, lax.rem(group, 2)
    middle = jnp.logical_or(me == 1, me == 2)
    twin = 2 * chip + 1 - core

    def peer(f):
        return 2 * lax.rem(chip + f % 4, 4) + lax.rem(core + f // 4, 2)

    def back(f):
        return f // 4 * 4 + (4 - f % 4) % 4

    def cols(p):
        return pl.ds(pl.multiple_of(p * part, 128), part)

    def z_peer(k):
        return lax.rem(me + k, owners)

    def send(src, dst, s, r, **where):
        return pltpu.make_async_remote_copy(
            src_ref=src,
            dst_ref=dst,
            send_sem=left.at[s],
            recv_sem=came.at[r],
            device_id=where,
            device_id_type=pl.DeviceIdType.MESH,
        )

    def arrived(dst, r):
        send(dst, dst, 0, r, dp=twin).wait_recv()

    def departed(src, s):
        send(src, src, s, 0, dp=twin).wait_send()

    barrier = pltpu.get_barrier_semaphore()
    for k in range(1, owners):
        pl.semaphore_signal(
            barrier, inc=1, device_id={"expert": z_peer(k)}, device_id_type=pl.DeviceIdType.MESH
        )
    for f in range(1, groups):
        pl.semaphore_signal(
            barrier, inc=1, device_id={"dp": peer(f)}, device_id_type=pl.DeviceIdType.MESH
        )
    small = [
        pltpu.make_async_copy(ids_hbm, ids_ref, load.at[4]),
        pltpu.make_async_copy(gate_hbm, gate_ref, load.at[5]),
        pltpu.make_async_copy(swapped_hbm, swapped_ref, load.at[6]),
    ]
    for copy in small:
        copy.start()
    loads = [
        pltpu.make_async_copy(tok_ref, xs.at[0], load.at[0]),
        pltpu.make_async_copy(og_ref, ogs.at[0], load.at[1]),
        pltpu.make_async_copy(up_ref.at[0], up_buf, load.at[2]),
        pltpu.make_async_copy(down_ref.at[0], down_buf, load.at[3]),
    ]
    for copy in loads:
        copy.start()
    for copy in small:
        copy.wait()
    lines = lax.broadcasted_iota(jnp.int32, (128, tok), 0)
    dense = jnp.zeros((128, tok), F32)
    for k in range(ids_ref.shape[0]):
        hit = ids_ref[k : k + 1, :] == lines
        dense += jnp.where(hit, gate_ref[k : k + 1, :].astype(F32), 0.0)
    eye = (
        lax.broadcasted_iota(jnp.int32, (128, 128), 0)
        == lax.broadcasted_iota(jnp.int32, (128, 128), 1)
    ).astype(BF)
    own_gates = dot(dense.astype(BF), eye, TN)
    gs[0] = own_gates.astype(BF)

    def column(v, e):
        lane = lax.broadcasted_iota(jnp.int32, v.shape, 1)
        return jnp.sum(jnp.where(lane == e, v, 0.0), axis=1, keepdims=True)

    def before(hits):
        rows = hits.shape[0]
        r = lax.broadcasted_iota(jnp.int32, (rows, rows), 0)
        c = lax.broadcasted_iota(jnp.int32, (rows, rows), 1)
        earlier = jnp.logical_and(c < r, c // tok == r // tok).astype(BF)
        return dot(earlier, hits.astype(BF))

    def named(gates, e, lanes):
        pick = lax.broadcasted_iota(jnp.int32, (128, lanes), 0) == e
        return (dot(gates, pick.astype(BF)) > 0).astype(F32)

    def packing(hits, turn):
        rank = before(hits)
        block = lax.broadcasted_iota(jnp.int32, hits.shape, 0) // tok
        block = ((block + turn) & 3).astype(F32)
        row = jnp.where(rank < 8, 8 * block + rank, 32 + 2 * block + rank - 8)
        lane = lax.broadcasted_iota(jnp.int32, hits.shape, 1).astype(F32)
        return jnp.where(lane == row, hits, 0.0).astype(BF)

    def fold(y, dst):
        for k in range(owners):
            rows = y[8 * k : 8 * k + 8]
            dst[k, :, :half] = jnp.concatenate([rows[:, :half], rows[:, half:]], axis=0).astype(BF)
        rest = jnp.concatenate(
            [y[32:40, eighth * j : eighth * (j + 1)] for j in range(8)], axis=0
        ).astype(BF)
        dst[:, :, half:] = dot(perm, rest).astype(BF).reshape(owners, tok, eighth)

    def unfold(src, dst):
        main = dot(main_pick, src[:, :, :half].reshape(count, half))
        rest = dot(rest_pick, src[:, :, half:].reshape(count, eighth))
        for q in range(8):
            h, at = q // 4, q % 4 * eighth
            dst[:, q * eighth : (q + 1) * eighth] = (
                main[tok * h : tok * (h + 1), at : at + eighth] + rest[tok * q : tok * (q + 1)]
            ).astype(BF)

    flag = swapped_ref[me]
    pl.semaphore_wait(barrier, owners + groups - 2)

    def gather(src, buf, s, r):
        for d, there in ((2, me < 2), (-2, me > 1), (1, me < 3), (-1, me > 0)):
            slot = -d % owners

            @pl.when(there)
            def _():
                send(
                    src, buf.at[slot], s, r + slot - 1, expert=lax.rem(me + d + owners, owners)
                ).start()

    def pass_on(buf, s, r):
        arrived(buf.at[2], r + 1)
        slot = 1 + 2 * lax.rem(me, 2)

        @pl.when(middle)
        def _():
            pltpu.make_async_remote_copy(
                src_ref=buf.at[2],
                dst_ref=buf.at[slot],
                send_sem=left.at[s],
                recv_sem=came.at[r + slot - 1],
                device_id={"expert": lax.rem(3 * (me + 3), owners)},
                device_id_type=pl.DeviceIdType.MESH,
            ).start()

    def spread_own(src, dst, s, r):
        for f in range(1, groups):
            p = peer(f)
            send(src.at[:, cols(p)], dst.at[back(f), 0], s, r, dp=p).start()

    rest = pl.ds(1, owners - 1)

    def spread_rest(buf, dst, s, r):
        for f in range(1, groups):
            p = peer(f)
            send(buf.at[rest, :, cols(p)], dst.at[back(f), rest], s, r, dp=p).start()
        dst[0, 1:] = buf[1:, :, cols(group)]

    for k in (2, 1, 3):
        send(gs.at[0], gs.at[owners - k], S_GATES, GATES, expert=z_peer(k)).start()
    gather(tok_ref, xs, S_X, X_IN)
    gather(og_ref, ogs, S_OG, OG_IN)
    spread_own(tok_ref, x_in, S_X_OWN, X_OWN)
    spread_own(og_ref, og_in, S_OG_OWN, OG_OWN)
    loads[3].wait()
    down_turned[...] = down_buf[...].T
    pass_on(xs, S_X_ON, X_IN)
    arrived(xs.at[1], X_IN)
    arrived(xs.at[3], X_IN + 2)
    loads[0].wait()
    x_in[0, 0] = xs[0, :, cols(group)]
    spread_rest(xs, x_in, S_X_REST, X_REST)
    pass_on(ogs, S_OG_ON, OG_IN)

    arrived(gs.at[rest], GATES)
    for f in range(1, groups):
        send(gs, gs_all.at[back(f)], S_GATES_ALL, GATES_ALL, dp=peer(f)).start()
    gs_all[0] = gs[...]
    gates = gs[...].reshape(count, 128)
    gate = column(gates.astype(F32), me)
    pack = packing(named(gates, me, room), 0)

    loads[2].wait()
    up = up_buf[...]
    hidden = dot(xs[...].reshape(count, width), up)
    sigma = 1.0 / (1.0 + jnp.exp(-hidden))
    active = (gate * (hidden * sigma)).astype(BF)
    slope = sigma * (1.0 + hidden * (1.0 - sigma))
    own_act[...] = dot(pack, active, TN).astype(BF)
    partner = lax.rem(me + 2, owners)
    send(own_act, other_act, S_SWAP_ACT, SWAP_ACT, expert=partner).start()
    spot = lax.broadcasted_iota(jnp.int32, (1, count), 1)
    own_hits = named(own_gates.astype(BF), (me + spot // tok) & 3, count)
    own_rank = before(own_hits)
    spot = (spot & (tok - 1)).astype(F32)
    low = jnp.where(own_rank < 8, own_hits, 0.0)
    high = own_hits - low
    main_pick = [jnp.where(spot == 8 * h + own_rank, low, 0.0) for h in range(2)]
    rest_pick = [jnp.where(spot == 2 * q + own_rank - 8, high, 0.0) for q in range(8)]
    main_pick = jnp.concatenate(main_pick, axis=0).astype(BF)
    rest_pick = jnp.concatenate(rest_pick, axis=0).astype(BF)
    c = lax.broadcasted_iota(jnp.int32, (count, count), 1)
    perm = (
        lax.broadcasted_iota(jnp.int32, (count, count), 0)
        == 16 * ((c >> 1) & 3) + 2 * (c >> 3) + (c & 1)
    ).astype(BF)

    down = down_buf[...]
    fold(dot(own_act[...], down), y_out)

    up_turned[...] = up.T
    arrived(ogs.at[1], OG_IN)
    arrived(ogs.at[3], OG_IN + 2)
    loads[1].wait()
    og_in[0, 0] = ogs[0, :, cols(group)]
    spread_rest(ogs, og_in, S_OG_REST, OG_REST)
    dy = (gate * ogs[...].reshape(count, width).astype(F32)).astype(BF)
    d_hidden = (dot(dy, down_turned[...]) * slope).astype(BF)
    own_dh[...] = dot(pack, d_hidden, TN).astype(BF)
    send(own_dh, other_dh, S_SWAP_DH, SWAP_DH, expert=partner).start()

    def send_back(out, into, s, r):
        for p in (0, 1, 2, 3):
            k = lax.rem(p + owners - me, owners)

            @pl.when(me != p)
            def _():
                send(
                    out.at[k], into.at[lax.rem(me + owners - p, owners)], s, r, expert=p
                ).start()

        into[0] = out[0]


    def choose(other, own, dst):
        dst[0] = jnp.where(flag == 1, other[...], own[...])

    def tell(buf, s, r, r_twin):
        for i in (2, 1, 3):
            send(buf.at[0], buf.at[4 - i], s, r + 3 - i, dp=peer(i)).start()
        send(buf.at[0], buf.at[4], s, r_twin, dp=twin).start()

    def tell_all(buf, s, r, r_twin):
        for f in (2, 6, 1, 3, 5, 7, 4):
            b = back(f)
            send(buf.at[0], buf.at[b], s, r + b - 1 if f < 4 else r_twin, dp=peer(f)).start()

    def heard(buf, r):
        for i in (1, 2, 3):
            arrived(buf.at[i], r + i - 1)

    def retell(buf, s, r, r_twin):
        for i in (1, 2, 3):
            arrived(buf.at[i], r + i - 1)
            send(buf.at[i], buf.at[4 + i], s, r_twin, dp=twin).start()

    arrived(other_act, SWAP_ACT)
    choose(other_act, own_act, act_all)
    tell(act_all, S_ACT, ACT_IN, ACT_TWIN)
    send_back(y_out, y_in, S_Y, Y)

    fold(dot(own_dh[...], up_turned[...]), dx_out)

    held = jnp.where(flag == 1, partner, me)
    others = pl.ds(1, groups - 1)
    arrived(gs_all.at[others], GATES_ALL)
    turn = jnp.where(flag == 1, 2, 0)
    hits = named(gs_all[...].reshape(groups * count, 128), held, room)
    packs = [packing(hits[count * f : count * (f + 1)], turn) for f in range(groups)]
    arrived(x_in.at[others, 0], X_OWN)
    arrived(x_in.at[others, rest], X_REST)
    for f in range(groups):
        x_rows[f] = dot(packs[f], x_in[f].reshape(count, part), TN).astype(BF)

    arrived(other_dh, SWAP_DH)
    choose(other_dh, own_dh, dh_all)
    tell_all(dh_all, S_DH, DH_IN, DH_TWIN)
    send_back(dx_out, dx_in, S_DX, DX)
    retell(act_all, S_ACT, ACT_IN, ACT_TWIN)

    total = groups * room
    arrived(og_in.at[others, 0], OG_OWN)
    arrived(og_in.at[others, rest], OG_REST)
    for f in range(groups):
        og_rows[f] = dot(packs[f], og_in[f].reshape(count, part), TN).astype(BF)
    arrived(act_all.at[pl.ds(4, 4)], ACT_TWIN)
    down_out[...] = (
        dot(act_all[...].reshape(total, fw), og_rows[...].reshape(total, part), TN)
        .astype(BF)
        .reshape(groups, depth, part)
    )
    for p in (0, 1, 2, 4, 6, 3, 5, 7):
        b, i = lax.rem(p + core, 2), lax.rem(p // 2 + 4 - chip, 4)

        @pl.when(group != p)
        def _():
            send(down_out.at[p], down_in.at[4 * b + lax.rem(4 - i, 4)], S_DOWN, DOWN, dp=p).start()

    down_in[0] = down_out[group]
    heard(dh_all, DH_IN)
    arrived(dh_all.at[pl.ds(4, 4)], DH_TWIN)
    ugrad_ref[0] = dot(x_rows[...].reshape(total, part), dh_all[...].reshape(total, fw), TN)

    arrived(y_in.at[rest], Y)
    unfold(y_in, out_ref)
    arrived(down_in.at[others], DOWN)
    for f in range(groups):
        dgrad_ref[0, :, cols(peer(f))] = down_in[f].astype(F32)
    arrived(dx_in.at[rest], DX)
    unfold(dx_in, tgrad_ref)

    for buf, s, s_on in ((xs, S_X, S_X_ON), (ogs, S_OG, S_OG_ON)):

        @pl.when(middle)
        def _():
            departed(buf.at[rest], s)
            departed(buf.at[0], s_on)

        @pl.when(jnp.logical_not(middle))
        def _():
            departed(buf.at[pl.ds(0, 2)], s)

    departed(gs.at[rest], S_GATES)
    departed(gs_all.at[others], S_GATES_ALL)
    departed(x_in.at[others, 0], S_X_OWN)
    departed(og_in.at[others, 0], S_OG_OWN)
    departed(x_in.at[others, rest], S_X_REST)
    departed(og_in.at[others, rest], S_OG_REST)
    departed(own_act, S_SWAP_ACT)
    departed(own_dh, S_SWAP_DH)
    departed(act_all.at[others], S_ACT)
    departed(dh_all.at[others], S_DH)
    departed(down_in.at[others], S_DOWN)
    departed(y_in.at[rest], S_Y)
    departed(dx_in.at[rest], S_DX)


def place(*refs):
    count = (len(refs) - 1) // 2
    copies = []
    for i in range(count):
        for j in range(2):
            rows = refs[i].shape[-2] // 2
            at = (0,) * (len(refs[i].shape) - 2) + (pl.ds(j * rows, rows),)
            copies.append(
                pltpu.make_async_copy(refs[i].at[at], refs[count + i].at[at], refs[-1].at[2 * i + j])
            )
    for copy in copies:
        copy.start()
    for copy in copies:
        copy.wait()


def by_kernel(groups, owners, tokens, out_grad, gate_weights, expert_ids, swapped, up, down):
    tok, width = tokens.shape
    fw = up.shape[2]
    part, depth, count = width // groups, fw // groups, owners * tok
    vmem = pl.BlockSpec(memory_space=pltpu.VMEM)
    hbm = pl.BlockSpec(memory_space=pltpu.HBM)
    dma = pltpu.SemaphoreType.DMA
    shapes = (
        ((tok, width), BF),
        ((tok, width), BF),
        ((1, part, fw), F32),
        ((1, depth, width), F32),
    )
    cut = pltpu.VMEM((groups, owners, tok, part), BF)
    room = 48
    hid = pltpu.VMEM((room, fw), BF)
    every = pltpu.VMEM((groups, room, fw), BF)
    folded = pltpu.VMEM((owners, tok, width // 2 + width // 8), BF)
    block = pltpu.VMEM((groups, depth, part), BF)
    params = pltpu.CompilerParams(
        collective_id=0, has_side_effects=True, vmem_limit_bytes=62 << 20
    )
    results = pl.pallas_call(
        kernel,
        out_shape=tuple(pltpu.VMEM(*a) for a in shapes),
        in_specs=[hbm] * 7,
        out_specs=(vmem,) * 4,
        scratch_shapes=[
            pltpu.VMEM((owners, tok, width), BF),
            pltpu.VMEM((owners, tok, width), BF),
            pltpu.VMEM((owners, tok, 128), BF),
            pltpu.VMEM((groups, owners, tok, 128), BF),
            pltpu.VMEM((groups, room, part), BF),
            pltpu.VMEM((groups, room, part), BF),
            pltpu.VMEM(up.shape[1:], BF),
            pltpu.VMEM(down.shape[1:], BF),
            pltpu.VMEM(up.shape[:0:-1], BF),
            pltpu.VMEM(down.shape[:0:-1], BF),
            cut,
            cut,
            hid,
            hid,
            hid,
            hid,
            every,
            every,
            folded,
            folded,
            folded,
            folded,
            block,
            block,
            pltpu.SMEM(swapped.shape, swapped.dtype),
            pltpu.VMEM(gate_weights.shape[::-1], BF),
            pltpu.VMEM(expert_ids.shape[::-1], jnp.int32),
            dma((7,)),
            dma((DEPARTURES,)),
            dma((ARRIVALS,)),
        ],
        compiler_params=params,
    )(swapped, tokens, out_grad, gate_weights.T, expert_ids.T, up, down)
    return pl.pallas_call(
        place,
        out_shape=tuple(jax.ShapeDtypeStruct(*a) for a in shapes),
        in_specs=[vmem] * 4,
        out_specs=(hbm,) * 4,
        scratch_shapes=[dma((8,))],
        compiler_params=pltpu.CompilerParams(vmem_limit_bytes=40 << 20),
    )(*results)


def solution(mesh):
    groups, owners = mesh.shape["dp"], mesh.shape["expert"]

    def on_device(tokens, out_grad, gate_weights, expert_ids, swapped, up_weight, down_weight):
        args = (tokens, out_grad, gate_weights, expert_ids, swapped, up_weight, down_weight)
        tok, width = tokens.shape
        fw = up_weight.shape[2]
        known = (groups, owners, tok, expert_ids.shape[1]) == (8, 4, 16, 2)
        if known and width % (128 * groups) == 0 and fw % (16 * groups) == 0:
            return by_kernel(groups, owners, *args)
        return by_collectives(*args)

    rows = P(("dp", "expert"), None)
    in_specs = (rows, rows, rows, rows, P(), P("expert", None, None), P("expert", None, None))
    out_specs = (rows, rows, P("expert", "dp", None), P("expert", "dp", None))
    return jax.shard_map(
        on_device, mesh=mesh, in_specs=in_specs, out_specs=out_specs, check_vma=False
    )
```
